512 devices in a mesh: dp: 128 (over z, y, core), mp: 4 (over x).
Axes of the slice: x: 4, y: 8, z: 8, core: 2. Of those that a mesh axis runs over, the one named last changes fastest.
Arguments:
- grads: bfloat16 [384, 512, 512], P(None, 'dp', 'mp'), may hold values from -6 to 6
- owner: int32 [384], replicated, may hold values from 0 to 127, as said below
- left_stat: float32 [384, 512, 512], P('dp', 'mp')
- right_stat: float32 [384, 512, 512], P('dp', 'mp')
- left_root: bfloat16 [384, 512, 512], P('dp', 'mp')
- right_root: bfloat16 [384, 512, 512], P('dp', 'mp')
Outputs:
- new_left: float32 [384, 512, 512], P('dp', 'mp')
- new_right: float32 [384, 512, 512], P('dp', 'mp')
- precond: bfloat16 [384, 512, 512], P(None, 'dp', 'mp')
The draws below stay inside these ranges and needn't reach their ends.
Inputs may be any that keep to these rules, and one draw needn't show every extreme that they name: Every owner index names exactly 3 blocks.
All inputs are finite; a program needn't handle non-finite values.
Results may differ from the reference program's by a relative error of at most 0.0049.
Values may be sent and summed in bfloat16 or wider, within the bound.
A program may use at most 64 MiB of HBM per device.

```python
import math
import jax
import jax.numpy as jnp
from jax import lax

BLOCK = 512
OWNED = 3
BLOCKS = 384


def dominant_matrix(key, spread, noise_scale):
    first_key, second_key = jax.random.split(key)
    diagonal = jnp.exp(jax.random.uniform(first_key, (BLOCKS, BLOCK, 1), jnp.float32, 0.0, math.log(spread)))
    identity = (jnp.arange(BLOCK)[:, None] == jnp.arange(BLOCK)[None, :]).astype(jnp.float32)
    noise = jax.random.normal(second_key, (BLOCKS, BLOCK, BLOCK), jnp.float32) * noise_scale
    return diagonal * identity + noise


def draw_owner(key, part):
    key = jax.random.fold_in(key, 1)
    shuffled = jax.random.permutation(key, jnp.arange(BLOCKS, dtype=jnp.int32))
    return (shuffled // OWNED).astype(jnp.int32)


def draw_left_stat(key, part):
    key = jax.random.fold_in(key, 2)
    return dominant_matrix(key, 4.0, 0.5 / math.sqrt(BLOCK))


def draw_right_stat(key, part):
    key = jax.random.fold_in(key, 3)
    return dominant_matrix(key, 4.0, 0.5 / math.sqrt(BLOCK))


def draw_left_root(key, part):
    key = jax.random.fold_in(key, 4)
    return dominant_matrix(key, 3.0, 0.4 / math.sqrt(BLOCK)).astype(jnp.bfloat16)


def draw_right_root(key, part):
    key = jax.random.fold_in(key, 5)
    return dominant_matrix(key, 3.0, 0.4 / math.sqrt(BLOCK)).astype(jnp.bfloat16)


def levels(own_key, extent, shards, smallest, top_value):
    factor_of = 1.0
    for position, blocks in shards:
        draws = jax.random.uniform(jax.random.fold_in(jax.random.fold_in(own_key, 6), position), (blocks,), jnp.float32, smallest / len(shards), top_value / len(shards))
        factor_of = factor_of * jnp.repeat(jnp.exp(draws), extent[position] // blocks).reshape((-1,) + (1,) * (len(extent) - 1 - position))
    return factor_of


def scatter_about(rng, dims, scale, reach, shards=(), kind=jnp.bfloat16):
    result = jax.random.normal(rng, dims, jnp.float32) * scale
    if len(shards) > 0:
        result = levels(rng, dims, shards, -0.22, 0.18) * result
    return jnp.clip(result, min=-reach, max=reach).astype(kind)


def setup_inputs(seed: int = 0) -> dict:
    seeds = jax.random.split(jax.random.key(seed), 7)
    grads = scatter_about(seeds[0], (BLOCKS, BLOCK, BLOCK), 1.0, 6.0, ((1, 128), (2, 4)))
    owner = draw_owner(jax.random.fold_in(seeds[6], 71), 0)
    left_stat = draw_left_stat(jax.random.fold_in(seeds[6], 71), 0)
    right_stat = draw_right_stat(jax.random.fold_in(seeds[6], 71), 0)
    left_root = draw_left_root(jax.random.fold_in(seeds[6], 71), 0)
    right_root = draw_right_root(jax.random.fold_in(seeds[6], 71), 0)
    return {"grads": grads, "owner": owner, "left_stat": left_stat, "right_stat": right_stat, "left_root": left_root, "right_root": right_root}


DECAY = 0.9
EPSILON = 1e-06

def reference(grads, owner, left_stat, right_stat, left_root, right_root):
    slot_order = jnp.argsort(owner, stable=True).astype(jnp.int32)

    def per_block(items):
        index, left_old, right_old, left_fac, right_fac = items
        gradient = lax.dynamic_index_in_dim(grads, index, 0, keepdims=False)
        outer_left = jnp.dot(gradient, gradient.T, preferred_element_type=jnp.float32)
        outer_right = jnp.dot(gradient.T, gradient, preferred_element_type=jnp.float32)
        left_next = DECAY * left_old + (1.0 - DECAY) / BLOCK * outer_left
        right_next = DECAY * right_old + (1.0 - DECAY) / BLOCK * outer_right
        half_way = jnp.dot(gradient, right_fac, preferred_element_type=jnp.float32).astype(jnp.bfloat16)
        product = jnp.dot(left_fac, half_way, preferred_element_type=jnp.float32)
        grad_wide = gradient.astype(jnp.float32)
        graft_scale = jnp.sqrt(jnp.sum(grad_wide * grad_wide) / (jnp.sum(product * product) + EPSILON))
        return (left_next, right_next, (product * graft_scale).astype(jnp.bfloat16))
    new_left, new_right, slotted = lax.map(per_block, (slot_order, left_stat, right_stat, left_root, right_root))
    inverse = jnp.argsort(slot_order).astype(jnp.int32)
    precond = jnp.take(slotted, inverse, axis=0)
    return (new_left, new_right, precond)
```

```python
import jax
import jax.numpy as jnp
from jax import lax
from jax.experimental import pallas as pl
from jax.experimental.pallas import tpu as pltpu
from jax.sharding import PartitionSpec as P

DECAY = 0.9
EPSILON = 1e-06
MESH = pl.DeviceIdType.MESH
F32 = jnp.float32
BF16 = jnp.bfloat16
SLOTS = 3
PLANES = 8
ROWMATES = 16
MEMBERS = 4
VIA_RIGHT = 64


def one_hot(condition):
    return jnp.where(condition, 1.0, 0.0).astype(BF16)


def iota(shape, dim):
    return lax.broadcasted_iota(jnp.int32, shape, dim)


def dot(a, b, contract=((1,), (0,))):
    return lax.dot_general(a, b, (contract, ((), ())), preferred_element_type=F32)


def across(row, tall):
    return jnp.concatenate(
        [one_hot(tall == row[:, 128 * t : 128 * t + 128]) for t in range(row.shape[1] // 128)], axis=1
    )


def sorted_block(index):
    slot, rowmate, plane = index >> 7, (index >> 3) & 15, index & 7
    return (plane * ROWMATES + rowmate) * SLOTS + slot


def kernel(
    grads_in, owner_in, left_stat, right_stat, left_root, right_root,
    new_left, new_right, precond,
    grads, owner, l_stat, r_stat, target, by_row, blocks, spread, stage,
    send_a, recv_a, send_b, g, roots, full, root_relay_0, root_relay_1, p, send_c, recv_c, send_d, recv_d, total,
    outer_send, outer_recv, outer_relay_0, outer_relay_1,
    local_sem, a_send, a_recv, b_send, b_recv, c_send, c_recv, d_send, d_recv,
    root_send, root_recv, root_relay_recv, outer_sent, outer_arrived, outer_relay_recv, members_in,
):
    d = lax.axis_index("dp")
    c = lax.axis_index("mp")
    plane = d // ROWMATES
    mate = d % ROWMATES
    right = lax.rem(c + 1, MEMBERS)
    left = lax.rem(c + MEMBERS - 1, MEMBERS)
    far = lax.rem(c + 2, MEMBERS)
    to_right, to_left = (d, right), (d, left)

    twice = 2 * lax.rem(d, 2)
    shift = lax.rem(twice + plane, MEMBERS)
    own_slot, right_slot, far_slot, left_slot = [lax.rem(c + i + MEMBERS - shift, MEMBERS) for i in range(MEMBERS)]

    def worker(k, owner_plane):
        return lax.rem(k + twice + owner_plane, MEMBERS)

    def far_first(j, count):
        return count // 2 + (j // 2) * (2 * (j % 2) - 1)

    def mate_at(j):
        other = lax.rem(mate + far_first(j, ROWMATES), ROWMATES)
        return other, plane * ROWMATES + other

    def plane_at(j):
        other = lax.rem(plane + far_first(j, PLANES), PLANES)
        return other, other * ROWMATES + mate

    def remote(src, dst, send, recv, device):
        return pltpu.make_async_remote_copy(
            src_ref=src, dst_ref=dst, send_sem=send, recv_sem=recv, device_id=device, device_id_type=MESH
        )

    def wait_bytes(ref, sem):
        pltpu.make_async_copy(ref, ref, sem).wait()

    def aligned(start, size):
        return pl.ds(pl.multiple_of(start, size), size)

    own = [
        pltpu.make_async_copy(owner_in, owner, local_sem.at[5]),
        pltpu.make_async_copy(grads_in, grads, local_sem.at[0]),
        pltpu.make_async_copy(left_root, roots.at[0], local_sem.at[1]),
        pltpu.make_async_copy(right_root, roots.at[1], local_sem.at[2]),
        pltpu.make_async_copy(left_stat, l_stat, local_sem.at[3]),
        pltpu.make_async_copy(right_stat, r_stat, local_sem.at[4]),
    ]
    for copy in own:
        copy.start()

    barrier = pltpu.get_barrier_semaphore()

    @pl.loop(1, ROWMATES, unroll=True)
    def _(j):
        pl.semaphore_signal(barrier, inc=1, device_id=(mate_at(j)[1], c), device_id_type=MESH)

    @pl.loop(1, MEMBERS, unroll=True)
    def _(j):
        pl.semaphore_signal(barrier, inc=1, device_id=(d, lax.rem(c + j, MEMBERS)), device_id_type=MESH)

    @pl.loop(1, PLANES, unroll=True)
    def _(j):
        pl.semaphore_signal(barrier, inc=1, device_id=(plane_at(j)[1], c), device_id_type=MESH)

    pl.semaphore_wait(barrier, ROWMATES + MEMBERS + PLANES - 3)

    def tell_column():
        @pl.loop(1, PLANES, unroll=True)
        def _(j):
            pl.semaphore_signal(members_in, inc=1, device_id=(plane_at(j)[1], c), device_id_type=MESH)

    top, bottom = pl.ds(0, VIA_RIGHT), pl.ds(VIA_RIGHT, 128 - VIA_RIGHT)

    def start_roots():
        @pl.when(far_slot < SLOTS)
        def _():
            remote(
                roots.at[:, far_slot, top], root_relay_0, root_send.at[2], root_relay_recv.at[0], to_right
            ).start()
            remote(
                roots.at[:, far_slot, bottom], root_relay_1, root_send.at[3], root_relay_recv.at[1], to_left
            ).start()

        @pl.when(right_slot < SLOTS)
        def _():
            remote(roots.at[:, right_slot], full.at[:, c], root_send.at[0], root_recv, to_right).start()

        @pl.when(left_slot < SLOTS)
        def _():
            remote(roots.at[:, left_slot], full.at[:, c], root_send.at[1], root_recv, to_left).start()

        @pl.when(own_slot < SLOTS)
        def _():
            full[:, c] = roots[:, own_slot]

    def pass_roots():
        @pl.when(right_slot < SLOTS)
        def _():
            wait_bytes(root_relay_0, root_relay_recv.at[0])
            remote(root_relay_0, full.at[:, left, top], root_send.at[4], root_recv, to_right).start()

        @pl.when(left_slot < SLOTS)
        def _():
            wait_bytes(root_relay_1, root_relay_recv.at[1])
            remote(root_relay_1, full.at[:, right, bottom], root_send.at[5], root_recv, to_left).start()

    def start_a(k):
        wanted = sorted_block(iota((128, 128), 0) + 128 * k).astype(F32)
        moved = dot(across(target[0:1, :], wanted), blocks[...])
        rows = [moved[:, 128 * i : 128 * i + 128].reshape(ROWMATES, 1, PLANES, 128) for i in range(4)]
        send_a[k] = jnp.concatenate(rows, axis=1).reshape(ROWMATES, 32, 128).astype(BF16)

        @pl.loop(1, ROWMATES, unroll=True)
        def _(j):
            other, device = mate_at(j)
            remote(send_a.at[k, other], recv_a.at[k, mate], a_send.at[k], a_recv.at[k], (device, c)).start()

        recv_a[k, mate] = send_a[k, mate]

    def start_b(k):
        wait_bytes(recv_a.at[k, pl.ds(0, ROWMATES - 1)], a_recv.at[k])
        stage[...] = recv_a[k].reshape(512, 128).astype(F32)
        for i in range(PLANES):
            send_b[k, i] = stage[pl.ds(i, 64, stride=PLANES), :].astype(BF16)
        member = worker(k, plane)
        place = c * PLANES + plane

        @pl.loop(1, PLANES, unroll=True)
        def _(j):
            other, device = plane_at(j)
            remote(send_b.at[k, other], g.at[place], b_send.at[k], b_recv, (device, worker(k, other))).start()

        @pl.when(member != c)
        def _():
            remote(send_b.at[k, plane], g.at[place], b_send.at[k], b_recv, (d, member)).start()

        @pl.when(member == c)
        def _():
            g[place] = send_b[k, plane]

    def gradient():
        parts = [g[pl.ds(PLANES * j, PLANES)].reshape(512, 128) for j in range(MEMBERS)]
        return jnp.concatenate(parts, axis=1)

    def work():
        wait_bytes(full.at[:, pl.ds(0, MEMBERS - 1)], root_recv)
        wait_bytes(g.at[pl.ds(0, PLANES * MEMBERS - 1)], b_recv)
        wide = gradient()
        half_way = dot(wide, full[1].reshape(512, 512)).astype(BF16)
        p[...] = dot(full[0].reshape(512, 512), half_way)
        grad_squares = jnp.zeros((1, 512), F32)
        product_squares = jnp.zeros((1, 512), F32)
        for i in range(4):
            part = wide[128 * i : 128 * i + 128].astype(F32)
            grad_squares = grad_squares + jnp.sum(part * part, axis=0, keepdims=True)
            part = p[pl.ds(128 * i, 128), :]
            product_squares = product_squares + jnp.sum(part * part, axis=0, keepdims=True)
        grad_squares = jnp.sum(grad_squares, axis=1, keepdims=True)
        product_squares = jnp.sum(product_squares, axis=1, keepdims=True)
        scale = jnp.sqrt(grad_squares / (product_squares + EPSILON))
        for j in range(MEMBERS):
            send_c[j] = (p[:, 128 * j : 128 * j + 128] * scale).astype(BF16).reshape(PLANES, 64, 128)

        def send(member, other):
            remote(
                send_c.at[member, other], recv_c.at[own_slot, plane],
                c_send, c_recv.at[own_slot], (other * ROWMATES + mate, member),
            ).start()

        @pl.loop(0, (PLANES - 1) * MEMBERS, unroll=True)
        def _(j):
            send(lax.rem(c + 2 + j % MEMBERS, MEMBERS), plane_at(j // MEMBERS + 1)[0])

        @pl.loop(1, MEMBERS, unroll=True)
        def _(j):
            send(lax.rem(c + j, MEMBERS), plane)

        recv_c[own_slot, plane] = send_c[c, plane]

    def outer_products():
        wide = gradient()
        outer_send[0] = dot(wide, wide, ((1,), (1,))).astype(BF16).reshape(MEMBERS, 128, 512)
        outer_send[1] = dot(wide, wide, ((0,), (0,))).astype(BF16).reshape(MEMBERS, 128, 512)
        remote(
            outer_send.at[:, far, top], outer_relay_0, outer_sent.at[2], outer_relay_recv.at[0], to_right
        ).start()
        remote(
            outer_send.at[:, far, bottom], outer_relay_1, outer_sent.at[3], outer_relay_recv.at[1], to_left
        ).start()
        for number, (member, device) in enumerate(((right, to_right), (left, to_left))):
            remote(
                outer_send.at[:, member], outer_recv.at[own_slot],
                outer_sent.at[number], outer_arrived.at[own_slot], device,
            ).start()
        outer_recv[own_slot] = outer_send[:, c]

    def pass_outer(k):
        @pl.when(left_slot == k)
        def _():
            wait_bytes(outer_relay_0, outer_relay_recv.at[0])
            remote(
                outer_relay_0, outer_recv.at[k, :, top],
                outer_sent.at[4], outer_arrived.at[k], to_right,
            ).start()

        @pl.when(right_slot == k)
        def _():
            wait_bytes(outer_relay_1, outer_relay_recv.at[1])
            remote(
                outer_relay_1, outer_recv.at[k, :, bottom],
                outer_sent.at[5], outer_arrived.at[k], to_left,
            ).start()

    def statistics(k):
        @pl.when(worker(k, plane) != c)
        def _():
            wait_bytes(outer_recv.at[k], outer_arrived.at[k])

        new_left[k] = DECAY * l_stat[k] + (1.0 - DECAY) / 512 * outer_recv[k, 0].astype(F32)
        new_right[k] = DECAY * r_stat[k] + (1.0 - DECAY) / 512 * outer_recv[k, 1].astype(F32)

    def start_d(k):
        @pl.when(worker(k, plane) != c)
        def _():
            wait_bytes(recv_c.at[k], c_recv.at[k])

        @pl.when(worker(k, plane) == c)
        def _():
            wait_bytes(recv_c.at[k, pl.ds(0, PLANES - 1)], c_recv.at[k])

        for i in range(PLANES):
            stage[pl.ds(i, 64, stride=PLANES), :] = recv_c[k, i].astype(F32)
        send_d[k] = stage[...].astype(BF16).reshape(ROWMATES, 32, 128)

        @pl.loop(1, ROWMATES, unroll=True)
        def _(j):
            other, device = mate_at(j)
            remote(send_d.at[k, other], recv_d.at[k, mate], d_send.at[k], d_recv.at[k], (device, c)).start()

        recv_d[k, mate] = send_d[k, mate]

    def finish(k):
        wait_bytes(recv_d.at[k, pl.ds(0, ROWMATES - 1)], d_recv.at[k])
        pieces = recv_d[k].astype(F32).reshape(ROWMATES, 4, PLANES, 128)
        pieces = jnp.concatenate([pieces[:, i].reshape(128, 128) for i in range(4)], axis=1).astype(BF16)
        part = dot(spread[:, 128 * k : 128 * k + 128], pieces)
        if k > 0:
            part = part + total[...]
        if k < SLOTS - 1:
            total[...] = part
        else:
            for i in range(4):
                by_row[pl.ds(i, 384, stride=4), :] = part[:, 128 * i : 128 * i + 128]
            precond[...] = by_row[...].astype(BF16)

    own[2].wait()
    own[3].wait()
    start_roots()

    own[0].wait()
    owned = jnp.concatenate([one_hot(owner[i : i + 1, :] == iota((128, 128), 0)) for i in range(3)], axis=1)
    earlier = iota((128, 384), 0).astype(F32) * SLOTS
    for i in range(3):
        earlier += dot(
            owned[:, 128 * i : 128 * i + 128], one_hot(iota((128, 384), 0) + 128 * i < iota((128, 384), 1))
        )
    number = jnp.sum(owned.astype(F32) * earlier, axis=0, keepdims=True)
    target[...] = jnp.broadcast_to(number, (8, 384))

    own[1].wait()
    by_row[...] = grads[...].astype(F32)
    for i in range(4):
        blocks[:, 128 * i : 128 * i + 128] = by_row[pl.ds(i, 384, stride=4), :].astype(BF16)
    start_a(0)
    tell_column()
    start_a(1)
    start_a(2)
    column = jnp.transpose(jnp.broadcast_to(target[0:1, :], (128, 384)))
    spread[...] = across(sorted_block(iota((1, 384), 1)).astype(F32), column)

    pl.semaphore_wait(members_in, PLANES - 1)
    start_b(0)
    pass_roots()
    start_b(1)
    start_b(2)
    for copy in own[4:]:
        copy.wait()
    pl.when(own_slot < SLOTS)(work)
    pl.when(own_slot < SLOTS)(outer_products)
    start_d(0)
    pass_outer(0)
    start_d(1)
    pass_outer(1)
    start_d(2)
    pass_outer(2)
    finish(0)
    finish(1)
    statistics(0)
    statistics(1)
    finish(2)
    statistics(2)

    for k in range(SLOTS):
        wait_bytes(send_a.at[k, pl.ds(0, ROWMATES - 1)], a_send.at[k])
        wait_bytes(send_d.at[k, pl.ds(0, ROWMATES - 1)], d_send.at[k])

        @pl.when(worker(k, plane) != c)
        def _():
            wait_bytes(send_b.at[k], b_send.at[k])

        @pl.when(worker(k, plane) == c)
        def _():
            wait_bytes(send_b.at[k, pl.ds(0, PLANES - 1)], b_send.at[k])

    @pl.when(own_slot < SLOTS)
    def _():
        wait_bytes(g.at[pl.ds(0, PLANES * MEMBERS - 1)], c_send)
        for i in range(2):
            wait_bytes(outer_recv.at[0], outer_sent.at[i])
        wait_bytes(outer_relay_0, outer_sent.at[2])
        wait_bytes(outer_relay_1, outer_sent.at[3])

    @pl.when(right_slot < SLOTS)
    def _():
        wait_bytes(full.at[:, 0], root_send.at[0])
        wait_bytes(root_relay_0, root_send.at[4])
        wait_bytes(outer_relay_1, outer_sent.at[5])

    @pl.when(left_slot < SLOTS)
    def _():
        wait_bytes(full.at[:, 0], root_send.at[1])
        wait_bytes(root_relay_1, root_send.at[5])
        wait_bytes(outer_relay_0, outer_sent.at[4])

    @pl.when(far_slot < SLOTS)
    def _():
        wait_bytes(root_relay_0, root_send.at[2])
        wait_bytes(root_relay_1, root_send.at[3])


def copy_kernel(*refs):
    sources, results, sem = refs[:3], refs[3:6], refs[6]
    copies = []
    for source, result in zip(sources, results):
        third = source.shape[0] // 3
        for i in range(3):
            rows = pl.ds(i * third, third)
            copies.append(pltpu.make_async_copy(source.at[rows], result.at[rows], sem.at[len(copies)]))
    for copy in copies:
        copy.start()
    for copy in copies:
        copy.wait()


def local(grads, owner, left_stat, right_stat, left_root, right_root):
    any_space = pl.BlockSpec(memory_space=pl.ANY)
    vmem = pl.BlockSpec(memory_space=pltpu.VMEM)
    dma = pltpu.SemaphoreType.DMA
    shapes = (
        jax.ShapeDtypeStruct((3, 128, 512), F32),
        jax.ShapeDtypeStruct((3, 128, 512), F32),
        jax.ShapeDtypeStruct((1536, 128), BF16),
    )
    results = pl.pallas_call(
        kernel,
        out_shape=tuple(pltpu.VMEM(x.shape, x.dtype) for x in shapes),
        in_specs=[any_space] * 6,
        out_specs=(vmem,) * 3,
        scratch_shapes=[
            pltpu.VMEM((1536, 128), BF16),
            pltpu.VMEM((3, 128), jnp.int32),
            pltpu.VMEM((3, 128, 512), F32),
            pltpu.VMEM((3, 128, 512), F32),
            pltpu.VMEM((8, 384), F32),
            pltpu.VMEM((1536, 128), F32),
            pltpu.VMEM((384, 512), BF16),
            pltpu.VMEM((384, 384), BF16),
            pltpu.VMEM((512, 128), F32),
            pltpu.VMEM((3, 16, 32, 128), BF16),
            pltpu.VMEM((3, 16, 32, 128), BF16),
            pltpu.VMEM((3, 8, 64, 128), BF16),
            pltpu.VMEM((32, 64, 128), BF16),
            pltpu.VMEM((2, 3, 128, 512), BF16),
            pltpu.VMEM((2, 4, 128, 512), BF16),
            pltpu.VMEM((2, VIA_RIGHT, 512), BF16),
            pltpu.VMEM((2, 128 - VIA_RIGHT, 512), BF16),
            pltpu.VMEM((512, 512), F32),
            pltpu.VMEM((4, 8, 64, 128), BF16),
            pltpu.VMEM((3, 8, 64, 128), BF16),
            pltpu.VMEM((3, 16, 32, 128), BF16),
            pltpu.VMEM((3, 16, 32, 128), BF16),
            pltpu.VMEM((384, 512), F32),
            pltpu.VMEM((2, 4, 128, 512), BF16),
            pltpu.VMEM((3, 2, 128, 512), BF16),
            pltpu.VMEM((2, VIA_RIGHT, 512), BF16),
            pltpu.VMEM((2, 128 - VIA_RIGHT, 512), BF16),
            dma((6,)),
            dma((3,)), dma((3,)),
            dma((3,)), dma,
            dma, dma((3,)),
            dma((3,)), dma((3,)),
            dma((6,)), dma, dma((2,)),
            dma((6,)), dma((3,)), dma((2,)),
            pltpu.SemaphoreType.REGULAR,
        ],
        compiler_params=pltpu.CompilerParams(
            collective_id=0, has_side_effects=True, vmem_limit_bytes=58 * 1024 * 1024
        ),
        cost_estimate=pl.CostEstimate(flops=4_000_000_000, bytes_accessed=6_000_000, transcendentals=0),
    )(grads.reshape(1536, 128), owner.reshape(3, 128), left_stat, right_stat, left_root, right_root)
    new_left, new_right, precond = pl.pallas_call(
        copy_kernel,
        out_shape=shapes,
        in_specs=[vmem] * 3,
        out_specs=(any_space,) * 3,
        scratch_shapes=[dma((9,))],
        compiler_params=pltpu.CompilerParams(vmem_limit_bytes=4 * 1024 * 1024),
        cost_estimate=pl.CostEstimate(flops=0, bytes_accessed=4_000_000, transcendentals=0),
    )(*results)
    return new_left, new_right, precond.reshape(384, 4, 128)


def solution(mesh):
    in_specs = (
        P(None, "dp", "mp"),
        P(),
        P("dp", "mp", None),
        P("dp", "mp", None),
        P("dp", "mp", None),
        P("dp", "mp", None),
    )
    out_specs = (P("dp", "mp", None), P("dp", "mp", None), P(None, "dp", "mp"))
    return jax.shard_map(local, mesh=mesh, in_specs=in_specs, out_specs=out_specs, check_vma=False)
```

```python
import jax
import jax.numpy as jnp
from jax import lax
from jax.experimental import pallas as pl
from jax.experimental.pallas import tpu as pltpu
from jax.sharding import PartitionSpec as P

DECAY = 0.9
EPSILON = 1e-06
MESH = pl.DeviceIdType.MESH
F32 = jnp.float32
BF16 = jnp.bfloat16
SLOTS = 3
PLANES = 8
ROWMATES = 16
MEMBERS = 4
VIA_RIGHT = 64


def one_hot(condition):
    return jnp.where(condition, 1.0, 0.0).astype(BF16)


def iota(shape, dim):
    return lax.broadcasted_iota(jnp.int32, shape, dim)


def dot(a, b, contract=((1,), (0,))):
    return lax.dot_general(a, b, (contract, ((), ())), preferred_element_type=F32)


def across(row, tall):
    return jnp.concatenate(
        [one_hot(tall == row[:, 128 * t : 128 * t + 128]) for t in range(row.shape[1] // 128)], axis=1
    )


def sorted_block(index):
    slot, rowmate, plane = index >> 7, (index >> 3) & 15, index & 7
    return (plane * ROWMATES + rowmate) * SLOTS + slot


def side_by_side(pieces):
    rows = pieces.astype(F32).reshape(ROWMATES, 4, PLANES, 128)
    return jnp.concatenate([rows[:, i].reshape(128, 128) for i in range(4)], axis=1).astype(BF16)


def kernel(
    grads_in, owner_in, left_stat, right_stat, left_root, right_root,
    new_left, new_right, total, last_spread, last_pieces,
    grads, owner, l_stat, r_stat, target, by_row, blocks, spread, stage,
    send_a, recv_a, send_b, g, roots, full, root_relay_0, root_relay_1, p, send_c, recv_c, send_d, recv_d,
    outer_send, outer_recv, outer_relay_0, outer_relay_1,
    local_sem, a_send, a_recv, b_send, b_recv, c_send, c_recv, d_send, d_recv,
    root_send, root_recv, root_relay_recv, outer_sent, outer_arrived, outer_relay_recv, members_in,
):
    d = lax.axis_index("dp")
    c = lax.axis_index("mp")
    plane = d // ROWMATES
    mate = d % ROWMATES
    right = lax.rem(c + 1, MEMBERS)
    left = lax.rem(c + MEMBERS - 1, MEMBERS)
    far = lax.rem(c + 2, MEMBERS)
    to_right, to_left = (d, right), (d, left)

    twice = 2 * lax.rem(d, 2)
    shift = lax.rem(twice + plane, MEMBERS)
    own_slot, right_slot, far_slot, left_slot = [lax.rem(c + i + MEMBERS - shift, MEMBERS) for i in range(MEMBERS)]

    def worker(k, owner_plane):
        return lax.rem(k + twice + owner_plane, MEMBERS)

    def far_first(j, count):
        return count // 2 + (j // 2) * (2 * (j % 2) - 1)

    def mate_at(j):
        other = lax.rem(mate + far_first(j, ROWMATES), ROWMATES)
        return other, plane * ROWMATES + other

    def plane_at(j):
        other = lax.rem(plane + far_first(j, PLANES), PLANES)
        return other, other * ROWMATES + mate

    def remote(src, dst, send, recv, device):
        return pltpu.make_async_remote_copy(
            src_ref=src, dst_ref=dst, send_sem=send, recv_sem=recv, device_id=device, device_id_type=MESH
        )

    def wait_bytes(ref, sem):
        pltpu.make_async_copy(ref, ref, sem).wait()

    def aligned(start, size):
        return pl.ds(pl.multiple_of(start, size), size)

    own = [
        pltpu.make_async_copy(owner_in, owner, local_sem.at[5]),
        pltpu.make_async_copy(grads_in, grads, local_sem.at[0]),
        pltpu.make_async_copy(left_root, roots.at[0], local_sem.at[1]),
        pltpu.make_async_copy(right_root, roots.at[1], local_sem.at[2]),
        pltpu.make_async_copy(left_stat, l_stat, local_sem.at[3]),
        pltpu.make_async_copy(right_stat, r_stat, local_sem.at[4]),
    ]
    for copy in own[:2]:
        copy.start()

    barrier = pltpu.get_barrier_semaphore()

    @pl.loop(1, ROWMATES, unroll=True)
    def _(j):
        pl.semaphore_signal(barrier, inc=1, device_id=(mate_at(j)[1], c), device_id_type=MESH)

    @pl.loop(1, MEMBERS, unroll=True)
    def _(j):
        pl.semaphore_signal(barrier, inc=1, device_id=(d, lax.rem(c + j, MEMBERS)), device_id_type=MESH)

    @pl.loop(1, PLANES, unroll=True)
    def _(j):
        pl.semaphore_signal(barrier, inc=1, device_id=(plane_at(j)[1], c), device_id_type=MESH)

    for copy in own[2:]:
        copy.start()

    def tell_column():
        @pl.loop(1, PLANES, unroll=True)
        def _(j):
            pl.semaphore_signal(members_in, inc=1, device_id=(plane_at(j)[1], c), device_id_type=MESH)

    top, bottom = pl.ds(0, VIA_RIGHT), pl.ds(VIA_RIGHT, 128 - VIA_RIGHT)

    def start_roots():
        @pl.when(far_slot < SLOTS)
        def _():
            remote(
                roots.at[:, far_slot, top], root_relay_0, root_send.at[2], root_relay_recv.at[0], to_right
            ).start()
            remote(
                roots.at[:, far_slot, bottom], root_relay_1, root_send.at[3], root_relay_recv.at[1], to_left
            ).start()

        @pl.when(right_slot < SLOTS)
        def _():
            remote(roots.at[:, right_slot], full.at[:, c], root_send.at[0], root_recv, to_right).start()

        @pl.when(left_slot < SLOTS)
        def _():
            remote(roots.at[:, left_slot], full.at[:, c], root_send.at[1], root_recv, to_left).start()

        @pl.when(own_slot < SLOTS)
        def _():
            full[:, c] = roots[:, own_slot]

    def pass_roots():
        @pl.when(right_slot < SLOTS)
        def _():
            wait_bytes(root_relay_0, root_relay_recv.at[0])
            remote(root_relay_0, full.at[:, left, top], root_send.at[4], root_recv, to_right).start()

        @pl.when(left_slot < SLOTS)
        def _():
            wait_bytes(root_relay_1, root_relay_recv.at[1])
            remote(root_relay_1, full.at[:, right, bottom], root_send.at[5], root_recv, to_left).start()

    def make_a(k):
        wanted = sorted_block(iota((128, 128), 0) + 128 * k).astype(F32)
        moved = dot(across(target[0:1, :], wanted), blocks[...])
        rows = [moved[:, 128 * i : 128 * i + 128].reshape(ROWMATES, 1, PLANES, 128) for i in range(4)]
        send_a[k] = jnp.concatenate(rows, axis=1).reshape(ROWMATES, 32, 128).astype(BF16)

    def start_a(k):
        @pl.loop(1, ROWMATES, unroll=True)
        def _(j):
            other, device = mate_at(j)
            remote(send_a.at[k, other], recv_a.at[k, mate], a_send.at[k], a_recv.at[k], (device, c)).start()

        recv_a[k, mate] = send_a[k, mate]

    def start_b(k):
        wait_bytes(recv_a.at[k, pl.ds(0, ROWMATES - 1)], a_recv.at[k])
        stage[...] = recv_a[k].reshape(512, 128).astype(F32)
        for i in range(PLANES):
            send_b[k, i] = stage[pl.ds(i, 64, stride=PLANES), :].astype(BF16)
        member = worker(k, plane)
        place = c * PLANES + plane

        @pl.loop(1, PLANES, unroll=True)
        def _(j):
            other, device = plane_at(j)
            remote(send_b.at[k, other], g.at[place], b_send.at[k], b_recv, (device, worker(k, other))).start()

        @pl.when(member != c)
        def _():
            remote(send_b.at[k, plane], g.at[place], b_send.at[k], b_recv, (d, member)).start()

        @pl.when(member == c)
        def _():
            g[place] = send_b[k, plane]

    def gradient():
        parts = [g[pl.ds(PLANES * j, PLANES)].reshape(512, 128) for j in range(MEMBERS)]
        return jnp.concatenate(parts, axis=1)

    def work():
        wait_bytes(full.at[:, pl.ds(0, MEMBERS - 1)], root_recv)
        wait_bytes(g.at[pl.ds(0, PLANES * MEMBERS - 1)], b_recv)
        wide = gradient()
        half_way = dot(wide, full[1].reshape(512, 512)).astype(BF16)
        p[...] = dot(full[0].reshape(512, 512), half_way)
        grad_squares = jnp.zeros((1, 512), F32)
        product_squares = jnp.zeros((1, 512), F32)
        for i in range(4):
            part = wide[128 * i : 128 * i + 128].astype(F32)
            grad_squares = grad_squares + jnp.sum(part * part, axis=0, keepdims=True)
            part = p[pl.ds(128 * i, 128), :]
            product_squares = product_squares + jnp.sum(part * part, axis=0, keepdims=True)
        grad_squares = jnp.sum(grad_squares, axis=1, keepdims=True)
        product_squares = jnp.sum(product_squares, axis=1, keepdims=True)
        scale = jnp.sqrt(grad_squares / (product_squares + EPSILON))
        for j in range(MEMBERS):
            send_c[j] = (p[:, 128 * j : 128 * j + 128] * scale).astype(BF16).reshape(PLANES, 64, 128)

        def send(member, other):
            remote(
                send_c.at[member, other], recv_c.at[own_slot, plane],
                c_send, c_recv.at[own_slot], (other * ROWMATES + mate, member),
            ).start()

        @pl.loop(0, (PLANES - 1) * MEMBERS, unroll=True)
        def _(j):
            send(lax.rem(c + 2 + j % MEMBERS, MEMBERS), plane_at(j // MEMBERS + 1)[0])

        @pl.loop(1, MEMBERS, unroll=True)
        def _(j):
            send(lax.rem(c + j, MEMBERS), plane)

        recv_c[own_slot, plane] = send_c[c, plane]

    def outer_products():
        wide = gradient()
        outer_send[0] = dot(wide, wide, ((1,), (1,))).astype(BF16).reshape(MEMBERS, 128, 512)
        outer_send[1] = dot(wide, wide, ((0,), (0,))).astype(BF16).reshape(MEMBERS, 128, 512)
        remote(
            outer_send.at[:, far, top], outer_relay_0, outer_sent.at[2], outer_relay_recv.at[0], to_right
        ).start()
        remote(
            outer_send.at[:, far, bottom], outer_relay_1, outer_sent.at[3], outer_relay_recv.at[1], to_left
        ).start()
        for number, (member, device) in enumerate(((right, to_right), (left, to_left))):
            remote(
                outer_send.at[:, member], outer_recv.at[own_slot],
                outer_sent.at[number], outer_arrived.at[own_slot], device,
            ).start()
        outer_recv[own_slot] = outer_send[:, c]

    def pass_outer(k):
        @pl.when(left_slot == k)
        def _():
            wait_bytes(outer_relay_0, outer_relay_recv.at[0])
            remote(
                outer_relay_0, outer_recv.at[k, :, top],
                outer_sent.at[4], outer_arrived.at[k], to_right,
            ).start()

        @pl.when(right_slot == k)
        def _():
            wait_bytes(outer_relay_1, outer_relay_recv.at[1])
            remote(
                outer_relay_1, outer_recv.at[k, :, bottom],
                outer_sent.at[5], outer_arrived.at[k], to_left,
            ).start()

    def statistics(k):
        @pl.when(worker(k, plane) != c)
        def _():
            wait_bytes(outer_recv.at[k], outer_arrived.at[k])

        new_left[k] = DECAY * l_stat[k] + (1.0 - DECAY) / 512 * outer_recv[k, 0].astype(F32)
        new_right[k] = DECAY * r_stat[k] + (1.0 - DECAY) / 512 * outer_recv[k, 1].astype(F32)

    def start_d(k):
        @pl.when(worker(k, plane) != c)
        def _():
            wait_bytes(recv_c.at[k], c_recv.at[k])

        @pl.when(worker(k, plane) == c)
        def _():
            wait_bytes(recv_c.at[k, pl.ds(0, PLANES - 1)], c_recv.at[k])

        for i in range(PLANES):
            stage[pl.ds(i, 64, stride=PLANES), :] = recv_c[k, i].astype(F32)
        send_d[k] = stage[...].astype(BF16).reshape(ROWMATES, 32, 128)

        @pl.loop(1, ROWMATES, unroll=True)
        def _(j):
            other, device = mate_at(j)
            remote(send_d.at[k, other], recv_d.at[k, mate], d_send.at[k], d_recv.at[k], (device, c)).start()

        recv_d[k, mate] = send_d[k, mate]

    def finish(k):
        wait_bytes(recv_d.at[k, pl.ds(0, ROWMATES - 1)], d_recv.at[k])
        part = dot(spread[:, 128 * k : 128 * k + 128], side_by_side(recv_d[k]))
        total[...] = part if k == 0 else part + total[...]

    own[0].wait()
    owned = jnp.concatenate([one_hot(owner[i : i + 1, :] == iota((128, 128), 0)) for i in range(3)], axis=1)
    earlier = iota((128, 384), 0).astype(F32) * SLOTS
    for i in range(3):
        earlier += dot(
            owned[:, 128 * i : 128 * i + 128], one_hot(iota((128, 384), 0) + 128 * i < iota((128, 384), 1))
        )
    number = jnp.sum(owned.astype(F32) * earlier, axis=0, keepdims=True)
    target[...] = jnp.broadcast_to(number, (8, 384))

    own[1].wait()
    by_row[...] = grads[...].astype(F32)
    for i in range(4):
        blocks[:, 128 * i : 128 * i + 128] = by_row[pl.ds(i, 384, stride=4), :].astype(BF16)
    make_a(0)
    pl.semaphore_wait(barrier, ROWMATES + MEMBERS + PLANES - 3)
    start_a(0)
    tell_column()
    own[2].wait()
    own[3].wait()
    start_roots()
    for k in (1, 2):
        make_a(k)
        start_a(k)
    column = jnp.transpose(jnp.broadcast_to(target[0:1, :], (128, 384)))
    spread[...] = across(sorted_block(iota((1, 384), 1)).astype(F32), column)

    pl.semaphore_wait(members_in, PLANES - 1)
    start_b(0)
    pass_roots()
    start_b(1)
    start_b(2)
    for copy in own[4:]:
        copy.wait()
    pl.when(own_slot < SLOTS)(work)
    pl.when(own_slot < SLOTS)(outer_products)
    start_d(0)
    pass_outer(0)
    start_d(1)
    pass_outer(1)
    start_d(2)
    pass_outer(2)
    finish(0)
    finish(1)
    statistics(0)
    statistics(1)
    last_spread[...] = spread[:, 256:384]
    wait_bytes(recv_d.at[2, pl.ds(0, ROWMATES - 1)], d_recv.at[2])
    last_pieces[...] = recv_d[2]
    statistics(2)

    for k in range(SLOTS):
        wait_bytes(send_a.at[k, pl.ds(0, ROWMATES - 1)], a_send.at[k])
        wait_bytes(send_d.at[k, pl.ds(0, ROWMATES - 1)], d_send.at[k])

        @pl.when(worker(k, plane) != c)
        def _():
            wait_bytes(send_b.at[k], b_send.at[k])

        @pl.when(worker(k, plane) == c)
        def _():
            wait_bytes(send_b.at[k, pl.ds(0, PLANES - 1)], b_send.at[k])

    @pl.when(own_slot < SLOTS)
    def _():
        wait_bytes(g.at[pl.ds(0, PLANES * MEMBERS - 1)], c_send)
        for i in range(2):
            wait_bytes(outer_recv.at[0], outer_sent.at[i])
        wait_bytes(outer_relay_0, outer_sent.at[2])
        wait_bytes(outer_relay_1, outer_sent.at[3])

    @pl.when(right_slot < SLOTS)
    def _():
        wait_bytes(full.at[:, 0], root_send.at[0])
        wait_bytes(root_relay_0, root_send.at[4])
        wait_bytes(outer_relay_1, outer_sent.at[5])

    @pl.when(left_slot < SLOTS)
    def _():
        wait_bytes(full.at[:, 0], root_send.at[1])
        wait_bytes(root_relay_1, root_send.at[5])
        wait_bytes(outer_relay_0, outer_sent.at[4])

    @pl.when(far_slot < SLOTS)
    def _():
        wait_bytes(root_relay_0, root_send.at[2])
        wait_bytes(root_relay_1, root_send.at[3])


def last_kernel(
    new_left, new_right, total, last_spread, last_pieces, left_out, right_out, precond_out, by_row, precond, sem
):
    copies = [
        pltpu.make_async_copy(source.at[k], result.at[k], sem.at[3 * i + k])
        for i, (source, result) in enumerate(((new_left, left_out), (new_right, right_out)))
        for k in range(SLOTS)
    ]
    for copy in copies:
        copy.start()
    blocks = total[...] + dot(last_spread[...], side_by_side(last_pieces[...]))
    for i in range(4):
        by_row[pl.ds(i, 384, stride=4), :] = blocks[:, 128 * i : 128 * i + 128]
    precond[...] = by_row[...].astype(BF16)
    copies.append(pltpu.make_async_copy(precond, precond_out, sem.at[6]))
    copies[-1].start()
    for copy in copies:
        copy.wait()


def local(grads, owner, left_stat, right_stat, left_root, right_root):
    any_space = pl.BlockSpec(memory_space=pl.ANY)
    vmem = pl.BlockSpec(memory_space=pltpu.VMEM)
    dma = pltpu.SemaphoreType.DMA
    results = pl.pallas_call(
        kernel,
        out_shape=(
            pltpu.VMEM((3, 128, 512), F32),
            pltpu.VMEM((3, 128, 512), F32),
            pltpu.VMEM((384, 512), F32),
            pltpu.VMEM((384, 128), BF16),
            pltpu.VMEM((16, 32, 128), BF16),
        ),
        in_specs=[any_space] * 6,
        out_specs=(vmem,) * 5,
        scratch_shapes=[
            pltpu.VMEM((1536, 128), BF16),
            pltpu.VMEM((3, 128), jnp.int32),
            pltpu.VMEM((3, 128, 512), F32),
            pltpu.VMEM((3, 128, 512), F32),
            pltpu.VMEM((8, 384), F32),
            pltpu.VMEM((1536, 128), F32),
            pltpu.VMEM((384, 512), BF16),
            pltpu.VMEM((384, 384), BF16),
            pltpu.VMEM((512, 128), F32),
            pltpu.VMEM((3, 16, 32, 128), BF16),
            pltpu.VMEM((3, 16, 32, 128), BF16),
            pltpu.VMEM((3, 8, 64, 128), BF16),
            pltpu.VMEM((32, 64, 128), BF16),
            pltpu.VMEM((2, 3, 128, 512), BF16),
            pltpu.VMEM((2, 4, 128, 512), BF16),
            pltpu.VMEM((2, VIA_RIGHT, 512), BF16),
            pltpu.VMEM((2, 128 - VIA_RIGHT, 512), BF16),
            pltpu.VMEM((512, 512), F32),
            pltpu.VMEM((4, 8, 64, 128), BF16),
            pltpu.VMEM((3, 8, 64, 128), BF16),
            pltpu.VMEM((3, 16, 32, 128), BF16),
            pltpu.VMEM((3, 16, 32, 128), BF16),
            pltpu.VMEM((2, 4, 128, 512), BF16),
            pltpu.VMEM((3, 2, 128, 512), BF16),
            pltpu.VMEM((2, VIA_RIGHT, 512), BF16),
            pltpu.VMEM((2, 128 - VIA_RIGHT, 512), BF16),
            dma((6,)),
            dma((3,)), dma((3,)),
            dma((3,)), dma,
            dma, dma((3,)),
            dma((3,)), dma((3,)),
            dma((6,)), dma, dma((2,)),
            dma((6,)), dma((3,)), dma((2,)),
            pltpu.SemaphoreType.REGULAR,
        ],
        compiler_params=pltpu.CompilerParams(
            collective_id=0, has_side_effects=True, vmem_limit_bytes=58 * 1024 * 1024
        ),
        cost_estimate=pl.CostEstimate(flops=4_000_000_000, bytes_accessed=6_000_000, transcendentals=0),
    )(grads.reshape(1536, 128), owner.reshape(3, 128), left_stat, right_stat, left_root, right_root)
    new_left, new_right, precond = pl.pallas_call(
        last_kernel,
        out_shape=(
            jax.ShapeDtypeStruct((3, 128, 512), F32),
            jax.ShapeDtypeStruct((3, 128, 512), F32),
            jax.ShapeDtypeStruct((1536, 128), BF16),
        ),
        in_specs=[vmem] * 5,
        out_specs=(any_space,) * 3,
        scratch_shapes=[pltpu.VMEM((1536, 128), F32), pltpu.VMEM((1536, 128), BF16), dma((7,))],
        compiler_params=pltpu.CompilerParams(vmem_limit_bytes=4 * 1024 * 1024),
        cost_estimate=pl.CostEstimate(flops=0, bytes_accessed=4_000_000, transcendentals=0),
    )(*results)
    return new_left, new_right, precond.reshape(384, 4, 128)


def solution(mesh):
    in_specs = (
        P(None, "dp", "mp"),
        P(),
        P("dp", "mp", None),
        P("dp", "mp", None),
        P("dp", "mp", None),
        P("dp", "mp", None),
    )
    out_specs = (P("dp", "mp", None), P("dp", "mp", None), P(None, "dp", "mp"))
    return jax.shard_map(local, mesh=mesh, in_specs=in_specs, out_specs=out_specs, check_vma=False)
```

```python
import jax
import jax.numpy as jnp
from jax import lax
from jax.experimental import pallas as pl
from jax.experimental.pallas import tpu as pltpu
from jax.sharding import PartitionSpec as P

DECAY = 0.9
EPSILON = 1e-06
MESH = pl.DeviceIdType.MESH
F32 = jnp.float32
BF16 = jnp.bfloat16
SLOTS = 3
PLANES = 8
ROWMATES = 16
MEMBERS = 4
VIA_RIGHT = 64


def one_hot(condition):
    return jnp.where(condition, 1.0, 0.0).astype(BF16)


def iota(shape, dim):
    return lax.broadcasted_iota(jnp.int32, shape, dim)


def dot(a, b, contract=((1,), (0,))):
    return lax.dot_general(a, b, (contract, ((), ())), preferred_element_type=F32)


def across(row, tall):
    return jnp.concatenate(
        [one_hot(tall == row[:, 128 * t : 128 * t + 128]) for t in range(row.shape[1] // 128)], axis=1
    )


def sorted_block(index):
    slot, rowmate, plane = index >> 7, (index >> 3) & 15, index & 7
    return (plane * ROWMATES + rowmate) * SLOTS + slot


def side_by_side(pieces):
    rows = pieces.astype(F32).reshape(ROWMATES, 4, PLANES, 128)
    return jnp.concatenate([rows[:, i].reshape(128, 128) for i in range(4)], axis=1).astype(BF16)


def kernel(
    grads_in, owner_in, left_stat, right_stat, left_root, right_root,
    new_left, new_right, total, last_spread, last_pieces,
    grads, owner, l_stat, r_stat, target, by_row, blocks, spread, stage,
    send_a, recv_a, send_b, g, roots, full, root_relay_0, root_relay_1, p, send_c, recv_c, send_d, recv_d,
    outer_send, outer_recv, outer_relay_0, outer_relay_1,
    local_sem, a_send, a_recv, b_send, b_recv, c_send, c_recv, d_send, d_recv,
    root_send, root_recv, root_relay_recv, outer_sent, outer_arrived, outer_relay_recv, members_in,
):
    d = lax.axis_index("dp")
    c = lax.axis_index("mp")
    plane = d // ROWMATES
    mate = d % ROWMATES
    right = lax.rem(c + 1, MEMBERS)
    left = lax.rem(c + MEMBERS - 1, MEMBERS)
    far = lax.rem(c + 2, MEMBERS)
    to_right, to_left = (d, right), (d, left)

    twice = 2 * lax.rem(d, 2)
    shift = lax.rem(twice + plane, MEMBERS)
    own_slot, right_slot, far_slot, left_slot = [lax.rem(c + i + MEMBERS - shift, MEMBERS) for i in range(MEMBERS)]

    def worker(k, owner_plane):
        return lax.rem(k + twice + owner_plane, MEMBERS)

    def far_first(j, count):
        return count // 2 + (j // 2) * (2 * (j % 2) - 1)

    def mate_at(j):
        other = lax.rem(mate + far_first(j, ROWMATES), ROWMATES)
        return other, plane * ROWMATES + other

    def plane_at(j):
        other = lax.rem(plane + far_first(j, PLANES), PLANES)
        return other, other * ROWMATES + mate

    def remote(src, dst, send, recv, device):
        return pltpu.make_async_remote_copy(
            src_ref=src, dst_ref=dst, send_sem=send, recv_sem=recv, device_id=device, device_id_type=MESH
        )

    def wait_bytes(ref, sem):
        pltpu.make_async_copy(ref, ref, sem).wait()

    def aligned(start, size):
        return pl.ds(pl.multiple_of(start, size), size)

    own = [
        pltpu.make_async_copy(owner_in, owner, local_sem.at[5]),
        pltpu.make_async_copy(grads_in, grads, local_sem.at[0]),
        pltpu.make_async_copy(left_root, roots.at[0], local_sem.at[1]),
        pltpu.make_async_copy(right_root, roots.at[1], local_sem.at[2]),
        pltpu.make_async_copy(left_stat, l_stat, local_sem.at[3]),
        pltpu.make_async_copy(right_stat, r_stat, local_sem.at[4]),
    ]
    for copy in own[:2]:
        copy.start()

    barrier = pltpu.get_barrier_semaphore()

    @pl.loop(1, ROWMATES, unroll=True)
    def _(j):
        pl.semaphore_signal(barrier, inc=1, device_id=(mate_at(j)[1], c), device_id_type=MESH)

    @pl.loop(1, MEMBERS, unroll=True)
    def _(j):
        pl.semaphore_signal(barrier, inc=1, device_id=(d, lax.rem(c + j, MEMBERS)), device_id_type=MESH)

    @pl.loop(1, PLANES, unroll=True)
    def _(j):
        pl.semaphore_signal(barrier, inc=1, device_id=(plane_at(j)[1], c), device_id_type=MESH)

    for copy in own[2:]:
        copy.start()

    def tell_column():
        @pl.loop(1, PLANES, unroll=True)
        def _(j):
            pl.semaphore_signal(members_in, inc=1, device_id=(plane_at(j)[1], c), device_id_type=MESH)

    top, bottom = pl.ds(0, VIA_RIGHT), pl.ds(VIA_RIGHT, 128 - VIA_RIGHT)

    def start_roots():
        @pl.when(far_slot < SLOTS)
        def _():
            remote(
                roots.at[:, far_slot, top], root_relay_0, root_send.at[2], root_relay_recv.at[0], to_right
            ).start()
            remote(
                roots.at[:, far_slot, bottom], root_relay_1, root_send.at[3], root_relay_recv.at[1], to_left
            ).start()

        @pl.when(right_slot < SLOTS)
        def _():
            remote(roots.at[:, right_slot], full.at[:, c], root_send.at[0], root_recv, to_right).start()

        @pl.when(left_slot < SLOTS)
        def _():
            remote(roots.at[:, left_slot], full.at[:, c], root_send.at[1], root_recv, to_left).start()

        @pl.when(own_slot < SLOTS)
        def _():
            full[:, c] = roots[:, own_slot]

    def pass_roots():
        @pl.when(right_slot < SLOTS)
        def _():
            wait_bytes(root_relay_0, root_relay_recv.at[0])
            remote(root_relay_0, full.at[:, left, top], root_send.at[4], root_recv, to_right).start()

        @pl.when(left_slot < SLOTS)
        def _():
            wait_bytes(root_relay_1, root_relay_recv.at[1])
            remote(root_relay_1, full.at[:, right, bottom], root_send.at[5], root_recv, to_left).start()

    def make_a(k):
        wanted = sorted_block(iota((128, 128), 0) + 128 * k).astype(F32)
        moved = dot(across(target[0:1, :], wanted), blocks[...])
        rows = [moved[:, 128 * i : 128 * i + 128].reshape(ROWMATES, 1, PLANES, 128) for i in range(4)]
        send_a[k] = jnp.concatenate(rows, axis=1).reshape(ROWMATES, 32, 128).astype(BF16)

    def start_a(k):
        @pl.loop(1, ROWMATES, unroll=True)
        def _(j):
            other, device = mate_at(j)
            remote(send_a.at[k, other], recv_a.at[k, mate], a_send.at[k], a_recv.at[k], (device, c)).start()

        recv_a[k, mate] = send_a[k, mate]

    def start_b(k):
        wait_bytes(recv_a.at[k, pl.ds(0, ROWMATES - 1)], a_recv.at[k])
        stage[...] = recv_a[k].reshape(512, 128).astype(F32)
        for i in range(PLANES):
            send_b[k, i] = stage[pl.ds(i, 64, stride=PLANES), :].astype(BF16)
        member = worker(k, plane)
        place = c * PLANES + plane

        @pl.loop(1, PLANES, unroll=True)
        def _(j):
            other, device = plane_at(j)
            remote(send_b.at[k, other], g.at[place], b_send.at[k], b_recv, (device, worker(k, other))).start()

        @pl.when(member != c)
        def _():
            remote(send_b.at[k, plane], g.at[place], b_send.at[k], b_recv, (d, member)).start()

        @pl.when(member == c)
        def _():
            g[place] = send_b[k, plane]

    def gradient():
        parts = [g[pl.ds(PLANES * j, PLANES)].reshape(512, 128) for j in range(MEMBERS)]
        return jnp.concatenate(parts, axis=1)

    def work():
        wait_bytes(full.at[:, pl.ds(0, MEMBERS - 1)], root_recv)
        wait_bytes(g.at[pl.ds(0, PLANES * MEMBERS - 1)], b_recv)
        wide = gradient()
        half_way = dot(wide, full[1].reshape(512, 512)).astype(BF16)
        p[...] = dot(full[0].reshape(512, 512), half_way)
        grad_squares = jnp.zeros((1, 512), F32)
        product_squares = jnp.zeros((1, 512), F32)
        for i in range(4):
            part = wide[128 * i : 128 * i + 128].astype(F32)
            grad_squares = grad_squares + jnp.sum(part * part, axis=0, keepdims=True)
            part = p[pl.ds(128 * i, 128), :]
            product_squares = product_squares + jnp.sum(part * part, axis=0, keepdims=True)
        grad_squares = jnp.sum(grad_squares, axis=1, keepdims=True)
        product_squares = jnp.sum(product_squares, axis=1, keepdims=True)
        scale = jnp.sqrt(grad_squares / (product_squares + EPSILON))
        for j in range(MEMBERS):
            send_c[j] = (p[:, 128 * j : 128 * j + 128] * scale).astype(BF16).reshape(PLANES, 64, 128)

        def send(member, other):
            remote(
                send_c.at[member, other], recv_c.at[own_slot, plane],
                c_send, c_recv.at[own_slot], (other * ROWMATES + mate, member),
            ).start()

        @pl.loop(0, (PLANES - 1) * MEMBERS, unroll=True)
        def _(j):
            send(lax.rem(c + 2 + j % MEMBERS, MEMBERS), plane_at(j // MEMBERS + 1)[0])

        @pl.loop(1, MEMBERS, unroll=True)
        def _(j):
            send(lax.rem(c + j, MEMBERS), plane)

        recv_c[own_slot, plane] = send_c[c, plane]

    def outer_products():
        wide = gradient()
        outer_send[0] = dot(wide, wide, ((1,), (1,))).astype(BF16).reshape(MEMBERS, 128, 512)
        outer_send[1] = dot(wide, wide, ((0,), (0,))).astype(BF16).reshape(MEMBERS, 128, 512)
        remote(
            outer_send.at[:, far, top], outer_relay_0, outer_sent.at[2], outer_relay_recv.at[0], to_right
        ).start()
        remote(
            outer_send.at[:, far, bottom], outer_relay_1, outer_sent.at[3], outer_relay_recv.at[1], to_left
        ).start()
        for number, (member, device) in enumerate(((right, to_right), (left, to_left))):
            remote(
                outer_send.at[:, member], outer_recv.at[own_slot],
                outer_sent.at[number], outer_arrived.at[own_slot], device,
            ).start()
        outer_recv[own_slot] = outer_send[:, c]

    def pass_outer(k):
        @pl.when(left_slot == k)
        def _():
            wait_bytes(outer_relay_0, outer_relay_recv.at[0])
            remote(
                outer_relay_0, outer_recv.at[k, :, top],
                outer_sent.at[4], outer_arrived.at[k], to_right,
            ).start()

        @pl.when(right_slot == k)
        def _():
            wait_bytes(outer_relay_1, outer_relay_recv.at[1])
            remote(
                outer_relay_1, outer_recv.at[k, :, bottom],
                outer_sent.at[5], outer_arrived.at[k], to_left,
            ).start()

    def statistics(k):
        @pl.when(worker(k, plane) != c)
        def _():
            wait_bytes(outer_recv.at[k], outer_arrived.at[k])

        new_left[k] = DECAY * l_stat[k] + (1.0 - DECAY) / 512 * outer_recv[k, 0].astype(F32)
        new_right[k] = DECAY * r_stat[k] + (1.0 - DECAY) / 512 * outer_recv[k, 1].astype(F32)

    def start_d(k):
        @pl.when(worker(k, plane) != c)
        def _():
            wait_bytes(recv_c.at[k], c_recv.at[k])

        @pl.when(worker(k, plane) == c)
        def _():
            wait_bytes(recv_c.at[k, pl.ds(0, PLANES - 1)], c_recv.at[k])

        for i in range(PLANES):
            stage[pl.ds(i, 64, stride=PLANES), :] = recv_c[k, i].astype(F32)
        send_d[k] = stage[...].astype(BF16).reshape(ROWMATES, 32, 128)

        @pl.loop(1, ROWMATES, unroll=True)
        def _(j):
            other, device = mate_at(j)
            remote(send_d.at[k, other], recv_d.at[k, mate], d_send.at[k], d_recv.at[k], (device, c)).start()

        recv_d[k, mate] = send_d[k, mate]

    def finish(k):
        wait_bytes(recv_d.at[k, pl.ds(0, ROWMATES - 1)], d_recv.at[k])
        part = dot(spread[:, 128 * k : 128 * k + 128], side_by_side(recv_d[k]))
        total[...] = part if k == 0 else part + total[...]

    own[0].wait()
    owned = jnp.concatenate([one_hot(owner[i : i + 1, :] == iota((128, 128), 0)) for i in range(3)], axis=1)
    earlier = iota((128, 384), 0).astype(F32) * SLOTS
    for i in range(3):
        earlier += dot(
            owned[:, 128 * i : 128 * i + 128], one_hot(iota((128, 384), 0) + 128 * i < iota((128, 384), 1))
        )
    number = jnp.sum(owned.astype(F32) * earlier, axis=0, keepdims=True)
    target[...] = jnp.broadcast_to(number, (8, 384))

    own[1].wait()
    by_row[...] = grads[...].astype(F32)
    for i in range(4):
        blocks[:, 128 * i : 128 * i + 128] = by_row[pl.ds(i, 384, stride=4), :].astype(BF16)
    make_a(0)
    own[2].wait()
    own[3].wait()
    pl.semaphore_wait(barrier, ROWMATES + MEMBERS + PLANES - 3)
    start_roots()
    start_a(0)
    tell_column()
    for k in (1, 2):
        make_a(k)
        start_a(k)
    column = jnp.transpose(jnp.broadcast_to(target[0:1, :], (128, 384)))
    spread[...] = across(sorted_block(iota((1, 384), 1)).astype(F32), column)

    pl.semaphore_wait(members_in, PLANES - 1)
    start_b(0)
    pass_roots()
    start_b(1)
    start_b(2)
    for copy in own[4:]:
        copy.wait()
    pl.when(own_slot < SLOTS)(work)
    pl.when(own_slot == SLOTS - 1)(outer_products)
    start_d(0)
    start_d(1)
    pl.when(own_slot < SLOTS - 1)(outer_products)
    start_d(2)
    for k in range(SLOTS):
        pass_outer(k)
    finish(0)
    finish(1)
    statistics(0)
    statistics(1)
    last_spread[...] = spread[:, 256:384]
    wait_bytes(recv_d.at[2, pl.ds(0, ROWMATES - 1)], d_recv.at[2])
    last_pieces[...] = recv_d[2]
    statistics(2)

    for k in range(SLOTS):
        wait_bytes(send_a.at[k, pl.ds(0, ROWMATES - 1)], a_send.at[k])
        wait_bytes(send_d.at[k, pl.ds(0, ROWMATES - 1)], d_send.at[k])

        @pl.when(worker(k, plane) != c)
        def _():
            wait_bytes(send_b.at[k], b_send.at[k])

        @pl.when(worker(k, plane) == c)
        def _():
            wait_bytes(send_b.at[k, pl.ds(0, PLANES - 1)], b_send.at[k])

    @pl.when(own_slot < SLOTS)
    def _():
        wait_bytes(g.at[pl.ds(0, PLANES * MEMBERS - 1)], c_send)
        for i in range(2):
            wait_bytes(outer_recv.at[0], outer_sent.at[i])
        wait_bytes(outer_relay_0, outer_sent.at[2])
        wait_bytes(outer_relay_1, outer_sent.at[3])

    @pl.when(right_slot < SLOTS)
    def _():
        wait_bytes(full.at[:, 0], root_send.at[0])
        wait_bytes(root_relay_0, root_send.at[4])
        wait_bytes(outer_relay_1, outer_sent.at[5])

    @pl.when(left_slot < SLOTS)
    def _():
        wait_bytes(full.at[:, 0], root_send.at[1])
        wait_bytes(root_relay_1, root_send.at[5])
        wait_bytes(outer_relay_0, outer_sent.at[4])

    @pl.when(far_slot < SLOTS)
    def _():
        wait_bytes(root_relay_0, root_send.at[2])
        wait_bytes(root_relay_1, root_send.at[3])


def last_kernel(
    new_left, new_right, total, last_spread, last_pieces, left_out, right_out, precond_out, by_row, precond, sem
):
    copies = [
        pltpu.make_async_copy(source.at[k], result.at[k], sem.at[3 * i + k])
        for i, (source, result) in enumerate(((new_left, left_out), (new_right, right_out)))
        for k in range(SLOTS)
    ]
    for copy in copies:
        copy.start()
    blocks = total[...] + dot(last_spread[...], side_by_side(last_pieces[...]))
    for i in range(4):
        by_row[pl.ds(i, 384, stride=4), :] = blocks[:, 128 * i : 128 * i + 128]
    precond[...] = by_row[...].astype(BF16)
    copies.append(pltpu.make_async_copy(precond, precond_out, sem.at[6]))
    copies[-1].start()
    for copy in copies:
        copy.wait()


def local(grads, owner, left_stat, right_stat, left_root, right_root):
    any_space = pl.BlockSpec(memory_space=pl.ANY)
    vmem = pl.BlockSpec(memory_space=pltpu.VMEM)
    dma = pltpu.SemaphoreType.DMA
    results = pl.pallas_call(
        kernel,
        out_shape=(
            pltpu.VMEM((3, 128, 512), F32),
            pltpu.VMEM((3, 128, 512), F32),
            pltpu.VMEM((384, 512), F32),
            pltpu.VMEM((384, 128), BF16),
            pltpu.VMEM((16, 32, 128), BF16),
        ),
        in_specs=[any_space] * 6,
        out_specs=(vmem,) * 5,
        scratch_shapes=[
            pltpu.VMEM((1536, 128), BF16),
            pltpu.VMEM((3, 128), jnp.int32),
            pltpu.VMEM((3, 128, 512), F32),
            pltpu.VMEM((3, 128, 512), F32),
            pltpu.VMEM((8, 384), F32),
            pltpu.VMEM((1536, 128), F32),
            pltpu.VMEM((384, 512), BF16),
            pltpu.VMEM((384, 384), BF16),
            pltpu.VMEM((512, 128), F32),
            pltpu.VMEM((3, 16, 32, 128), BF16),
            pltpu.VMEM((3, 16, 32, 128), BF16),
            pltpu.VMEM((3, 8, 64, 128), BF16),
            pltpu.VMEM((32, 64, 128), BF16),
            pltpu.VMEM((2, 3, 128, 512), BF16),
            pltpu.VMEM((2, 4, 128, 512), BF16),
            pltpu.VMEM((2, VIA_RIGHT, 512), BF16),
            pltpu.VMEM((2, 128 - VIA_RIGHT, 512), BF16),
            pltpu.VMEM((512, 512), F32),
            pltpu.VMEM((4, 8, 64, 128), BF16),
            pltpu.VMEM((3, 8, 64, 128), BF16),
            pltpu.VMEM((3, 16, 32, 128), BF16),
            pltpu.VMEM((3, 16, 32, 128), BF16),
            pltpu.VMEM((2, 4, 128, 512), BF16),
            pltpu.VMEM((3, 2, 128, 512), BF16),
            pltpu.VMEM((2, VIA_RIGHT, 512), BF16),
            pltpu.VMEM((2, 128 - VIA_RIGHT, 512), BF16),
            dma((6,)),
            dma((3,)), dma((3,)),
            dma((3,)), dma,
            dma, dma((3,)),
            dma((3,)), dma((3,)),
            dma((6,)), dma, dma((2,)),
            dma((6,)), dma((3,)), dma((2,)),
            pltpu.SemaphoreType.REGULAR,
        ],
        compiler_params=pltpu.CompilerParams(
            collective_id=0, has_side_effects=True, vmem_limit_bytes=58 * 1024 * 1024
        ),
        cost_estimate=pl.CostEstimate(flops=4_000_000_000, bytes_accessed=6_000_000, transcendentals=0),
    )(grads.reshape(1536, 128), owner.reshape(3, 128), left_stat, right_stat, left_root, right_root)
    new_left, new_right, precond = pl.pallas_call(
        last_kernel,
        out_shape=(
            jax.ShapeDtypeStruct((3, 128, 512), F32),
            jax.ShapeDtypeStruct((3, 128, 512), F32),
            jax.ShapeDtypeStruct((1536, 128), BF16),
        ),
        in_specs=[vmem] * 5,
        out_specs=(any_space,) * 3,
        scratch_shapes=[pltpu.VMEM((1536, 128), F32), pltpu.VMEM((1536, 128), BF16), dma((7,))],
        compiler_params=pltpu.CompilerParams(vmem_limit_bytes=4 * 1024 * 1024),
        cost_estimate=pl.CostEstimate(flops=0, bytes_accessed=4_000_000, transcendentals=0),
    )(*results)
    return new_left, new_right, precond.reshape(384, 4, 128)


def solution(mesh):
    in_specs = (
        P(None, "dp", "mp"),
        P(),
        P("dp", "mp", None),
        P("dp", "mp", None),
        P("dp", "mp", None),
        P("dp", "mp", None),
    )
    out_specs = (P("dp", "mp", None), P("dp", "mp", None), P(None, "dp", "mp"))
    return jax.shard_map(local, mesh=mesh, in_specs=in_specs, out_specs=out_specs, check_vma=False)
```

```python
import jax
import jax.numpy as jnp
from jax import lax
from jax.experimental import pallas as pl
from jax.experimental.pallas import tpu as pltpu
from jax.sharding import PartitionSpec as P

DECAY = 0.9
EPSILON = 1e-06
MESH = pl.DeviceIdType.MESH
F32 = jnp.float32
BF16 = jnp.bfloat16
SLOTS = 3
HALVES = 2
PLANES = 8
ROWMATES = 16
MEMBERS = 4
VIA_RIGHT = 64


def one_hot(condition):
    return jnp.where(condition, 1.0, 0.0).astype(BF16)


def iota(shape, dim):
    return lax.broadcasted_iota(jnp.int32, shape, dim)


def dot(a, b, contract=((1,), (0,))):
    return lax.dot_general(a, b, (contract, ((), ())), preferred_element_type=F32)


def across(row, tall):
    return jnp.concatenate(
        [one_hot(tall == row[:, 128 * t : 128 * t + 128]) for t in range(row.shape[1] // 128)], axis=1
    )


def sorted_block(index):
    slot, rowmate, plane = index >> 7, (index >> 3) & 15, index & 7
    return (plane * ROWMATES + rowmate) * SLOTS + slot


def side_by_side(pieces):
    rows = pieces.astype(F32).reshape(ROWMATES, 4, PLANES, 128)
    return jnp.concatenate([rows[:, i].reshape(128, 128) for i in range(4)], axis=1).astype(BF16)


def kernel(
    grads_in, owner_in, left_stat, right_stat, left_root, right_root,
    new_left, new_right, total, last_spread, last_pieces,
    grads, owner, l_stat, r_stat, target, by_row, blocks, spread, stage,
    send_a, recv_a, send_b, g, roots, full, root_relay_0, root_relay_1, p, send_c, recv_c, send_d, recv_d,
    outer_send, outer_recv, outer_relay_0, outer_relay_1,
    local_sem, a_send, a_recv, b_send, b_recv, c_send, c_recv, d_send, d_recv,
    root_send, root_recv, root_relay_recv, outer_sent, outer_arrived, outer_relay_recv, members_in,
):
    d = lax.axis_index("dp")
    c = lax.axis_index("mp")
    plane = d // ROWMATES
    mate = d % ROWMATES
    right = lax.rem(c + 1, MEMBERS)
    left = lax.rem(c + MEMBERS - 1, MEMBERS)
    far = lax.rem(c + 2, MEMBERS)
    to_right, to_left = (d, right), (d, left)

    twice = 2 * lax.rem(d, 2)
    shift = lax.rem(twice + plane, MEMBERS)
    own_slot, right_slot, far_slot, left_slot = [lax.rem(c + i + MEMBERS - shift, MEMBERS) for i in range(MEMBERS)]

    def worker(k, owner_plane):
        return lax.rem(k + twice + owner_plane, MEMBERS)

    def far_first(j, count):
        return count // 2 + (j // 2) * (2 * (j % 2) - 1)

    def mate_at(j):
        other = lax.rem(mate + far_first(j, ROWMATES), ROWMATES)
        return other, plane * ROWMATES + other

    def plane_at(j):
        other = lax.rem(plane + far_first(j, PLANES), PLANES)
        return other, other * ROWMATES + mate

    def remote(src, dst, send, recv, device):
        return pltpu.make_async_remote_copy(
            src_ref=src, dst_ref=dst, send_sem=send, recv_sem=recv, device_id=device, device_id_type=MESH
        )

    def wait_bytes(ref, sem):
        pltpu.make_async_copy(ref, ref, sem).wait()

    def aligned(start, size):
        return pl.ds(pl.multiple_of(start, size), size)

    own = [
        pltpu.make_async_copy(owner_in, owner, local_sem.at[5]),
        pltpu.make_async_copy(grads_in, grads, local_sem.at[0]),
        pltpu.make_async_copy(left_root, roots.at[0], local_sem.at[1]),
        pltpu.make_async_copy(right_root, roots.at[1], local_sem.at[2]),
        pltpu.make_async_copy(left_stat, l_stat, local_sem.at[3]),
        pltpu.make_async_copy(right_stat, r_stat, local_sem.at[4]),
    ]
    for copy in own[:2]:
        copy.start()

    barrier = pltpu.get_barrier_semaphore()

    @pl.loop(1, ROWMATES, unroll=True)
    def _(j):
        pl.semaphore_signal(barrier, inc=1, device_id=(mate_at(j)[1], c), device_id_type=MESH)

    @pl.loop(1, MEMBERS, unroll=True)
    def _(j):
        pl.semaphore_signal(barrier, inc=1, device_id=(d, lax.rem(c + j, MEMBERS)), device_id_type=MESH)

    @pl.loop(1, PLANES, unroll=True)
    def _(j):
        pl.semaphore_signal(barrier, inc=1, device_id=(plane_at(j)[1], c), device_id_type=MESH)

    for copy in own[2:]:
        copy.start()

    def tell_column():
        @pl.loop(1, PLANES, unroll=True)
        def _(j):
            pl.semaphore_signal(members_in, inc=1, device_id=(plane_at(j)[1], c), device_id_type=MESH)

    top, bottom = pl.ds(0, VIA_RIGHT), pl.ds(VIA_RIGHT, 128 - VIA_RIGHT)

    def start_roots():
        @pl.when(far_slot < SLOTS)
        def _():
            remote(
                roots.at[:, far_slot, top], root_relay_0, root_send.at[2], root_relay_recv.at[0], to_right
            ).start()
            remote(
                roots.at[:, far_slot, bottom], root_relay_1, root_send.at[3], root_relay_recv.at[1], to_left
            ).start()

        @pl.when(right_slot < SLOTS)
        def _():
            remote(roots.at[:, right_slot], full.at[:, c], root_send.at[0], root_recv, to_right).start()

        @pl.when(left_slot < SLOTS)
        def _():
            remote(roots.at[:, left_slot], full.at[:, c], root_send.at[1], root_recv, to_left).start()

        @pl.when(own_slot < SLOTS)
        def _():
            full[:, c] = roots[:, own_slot]

    def pass_roots():
        @pl.when(right_slot < SLOTS)
        def _():
            wait_bytes(root_relay_0, root_relay_recv.at[0])
            remote(root_relay_0, full.at[:, left, top], root_send.at[4], root_recv, to_right).start()

        @pl.when(left_slot < SLOTS)
        def _():
            wait_bytes(root_relay_1, root_relay_recv.at[1])
            remote(root_relay_1, full.at[:, right, bottom], root_send.at[5], root_recv, to_left).start()

    def make_a(k):
        wanted = sorted_block(iota((128, 128), 0) + 128 * k).astype(F32)
        moved = dot(across(target[0:1, :], wanted), blocks[...])
        rows = [moved[:, 128 * i : 128 * i + 128].reshape(ROWMATES, 1, PLANES, 128) for i in range(4)]
        send_a[k] = jnp.concatenate(rows, axis=1).reshape(ROWMATES, 32, 128).astype(BF16)

    def start_a(k):
        @pl.loop(1, ROWMATES, unroll=True)
        def _(j):
            other, device = mate_at(j)
            remote(send_a.at[k, other], recv_a.at[k, mate], a_send.at[k], a_recv.at[k], (device, c)).start()

        recv_a[k, mate] = send_a[k, mate]

    def start_b(k):
        wait_bytes(recv_a.at[k, pl.ds(0, ROWMATES - 1)], a_recv.at[k])
        stage[...] = recv_a[k].reshape(512, 128).astype(F32)
        for i in range(PLANES):
            send_b[k, i] = stage[pl.ds(i, 64, stride=PLANES), :].astype(BF16)
        member = worker(k, plane)
        place = c * PLANES + plane

        @pl.loop(1, PLANES, unroll=True)
        def _(j):
            other, device = plane_at(j)
            remote(send_b.at[k, other], g.at[place], b_send.at[k], b_recv, (device, worker(k, other))).start()

        @pl.when(member != c)
        def _():
            remote(send_b.at[k, plane], g.at[place], b_send.at[k], b_recv, (d, member)).start()

        @pl.when(member == c)
        def _():
            g[place] = send_b[k, plane]

    def gradient():
        parts = [g[pl.ds(PLANES * j, PLANES)].reshape(512, 128) for j in range(MEMBERS)]
        return jnp.concatenate(parts, axis=1)

    def work():
        wait_bytes(full.at[:, pl.ds(0, MEMBERS - 1)], root_recv)
        wait_bytes(g.at[pl.ds(0, PLANES * MEMBERS - 1)], b_recv)
        wide = gradient()
        half_way = dot(wide, full[1].reshape(512, 512)).astype(BF16)
        p[...] = dot(full[0].reshape(512, 512), half_way)
        grad_squares = jnp.zeros((1, 512), F32)
        product_squares = jnp.zeros((1, 512), F32)
        for i in range(4):
            part = wide[128 * i : 128 * i + 128].astype(F32)
            grad_squares = grad_squares + jnp.sum(part * part, axis=0, keepdims=True)
            part = p[pl.ds(128 * i, 128), :]
            product_squares = product_squares + jnp.sum(part * part, axis=0, keepdims=True)
        grad_squares = jnp.sum(grad_squares, axis=1, keepdims=True)
        product_squares = jnp.sum(product_squares, axis=1, keepdims=True)
        scale = jnp.sqrt(grad_squares / (product_squares + EPSILON))
        for j in range(MEMBERS):
            send_c[j] = (p[:, 128 * j : 128 * j + 128] * scale).astype(BF16).reshape(PLANES, 64, 128)

        for half in range(HALVES):
            rows = pl.ds(32 * half, 32)

            def send(member, other):
                remote(
                    send_c.at[member, other, rows], recv_c.at[own_slot, plane, rows],
                    c_send, c_recv.at[own_slot, half], (other * ROWMATES + mate, member),
                ).start()

            @pl.loop(0, (PLANES - 1) * MEMBERS, unroll=True)
            def _(j):
                send(lax.rem(c + 2 + j % MEMBERS, MEMBERS), plane_at(j // MEMBERS + 1)[0])

            @pl.loop(1, MEMBERS, unroll=True)
            def _(j):
                send(lax.rem(c + j, MEMBERS), plane)

        recv_c[own_slot, plane] = send_c[c, plane]

    def outer_products():
        wide = gradient()
        outer_send[0] = dot(wide, wide, ((1,), (1,))).astype(BF16).reshape(MEMBERS, 128, 512)
        outer_send[1] = dot(wide, wide, ((0,), (0,))).astype(BF16).reshape(MEMBERS, 128, 512)
        remote(
            outer_send.at[:, far, top], outer_relay_0, outer_sent.at[2], outer_relay_recv.at[0], to_right
        ).start()
        remote(
            outer_send.at[:, far, bottom], outer_relay_1, outer_sent.at[3], outer_relay_recv.at[1], to_left
        ).start()
        for number, (member, device) in enumerate(((right, to_right), (left, to_left))):
            remote(
                outer_send.at[:, member], outer_recv.at[own_slot],
                outer_sent.at[number], outer_arrived.at[own_slot], device,
            ).start()
        outer_recv[own_slot] = outer_send[:, c]

    def pass_outer(k):
        @pl.when(left_slot == k)
        def _():
            wait_bytes(outer_relay_0, outer_relay_recv.at[0])
            remote(
                outer_relay_0, outer_recv.at[k, :, top],
                outer_sent.at[4], outer_arrived.at[k], to_right,
            ).start()

        @pl.when(right_slot == k)
        def _():
            wait_bytes(outer_relay_1, outer_relay_recv.at[1])
            remote(
                outer_relay_1, outer_recv.at[k, :, bottom],
                outer_sent.at[5], outer_arrived.at[k], to_left,
            ).start()

    def statistics(k):
        @pl.when(worker(k, plane) != c)
        def _():
            wait_bytes(outer_recv.at[k], outer_arrived.at[k])

        new_left[k] = DECAY * l_stat[k] + (1.0 - DECAY) / 512 * outer_recv[k, 0].astype(F32)
        new_right[k] = DECAY * r_stat[k] + (1.0 - DECAY) / 512 * outer_recv[k, 1].astype(F32)

    def start_d(k):
        for half in range(HALVES):
            rows = pl.ds(32 * half, 32)

            @pl.when(worker(k, plane) != c)
            def _():
                wait_bytes(recv_c.at[k, :, rows], c_recv.at[k, half])

            @pl.when(worker(k, plane) == c)
            def _():
                wait_bytes(recv_c.at[k, pl.ds(0, PLANES - 1), rows], c_recv.at[k, half])

            for i in range(PLANES):
                stage[pl.ds(i, 32, stride=PLANES), :] = recv_c[k, i, rows].astype(F32)
            send_d[k, pl.ds(8 * half, 8)] = stage[pl.ds(0, 256), :].astype(BF16).reshape(8, 32, 128)

            @pl.loop(0, 8, unroll=True)
            def _(j):
                other = 8 * half + lax.rem(mate + 4 + j, 8)

                @pl.when(other != mate)
                def _():
                    device = (plane * ROWMATES + other, c)
                    remote(send_d.at[k, other], recv_d.at[k, mate], d_send.at[k], d_recv.at[k], device).start()

        recv_d[k, mate] = send_d[k, mate]

    def finish(k):
        wait_bytes(recv_d.at[k, pl.ds(0, ROWMATES - 1)], d_recv.at[k])
        part = dot(spread[:, 128 * k : 128 * k + 128], side_by_side(recv_d[k]))
        total[...] = part if k == 0 else part + total[...]

    own[0].wait()
    owned = jnp.concatenate([one_hot(owner[i : i + 1, :] == iota((128, 128), 0)) for i in range(3)], axis=1)
    earlier = iota((128, 384), 0).astype(F32) * SLOTS
    for i in range(3):
        earlier += dot(
            owned[:, 128 * i : 128 * i + 128], one_hot(iota((128, 384), 0) + 128 * i < iota((128, 384), 1))
        )
    number = jnp.sum(owned.astype(F32) * earlier, axis=0, keepdims=True)
    target[...] = jnp.broadcast_to(number, (8, 384))

    own[1].wait()
    by_row[...] = grads[...].astype(F32)
    for i in range(4):
        blocks[:, 128 * i : 128 * i + 128] = by_row[pl.ds(i, 384, stride=4), :].astype(BF16)
    make_a(0)
    own[2].wait()
    own[3].wait()
    pl.semaphore_wait(barrier, ROWMATES + MEMBERS + PLANES - 3)
    start_roots()
    start_a(0)
    tell_column()
    for k in (1, 2):
        make_a(k)
        start_a(k)
    column = jnp.transpose(jnp.broadcast_to(target[0:1, :], (128, 384)))
    spread[...] = across(sorted_block(iota((1, 384), 1)).astype(F32), column)

    pl.semaphore_wait(members_in, PLANES - 1)
    start_b(0)
    pass_roots()
    start_b(1)
    start_b(2)
    for copy in own[4:]:
        copy.wait()
    pl.when(own_slot < SLOTS)(work)
    pl.when(own_slot < SLOTS)(outer_products)
    for k in range(SLOTS):
        start_d(k)
        pass_outer(k)
    finish(0)
    finish(1)
    statistics(0)
    statistics(1)
    last_spread[...] = spread[:, 256:384]
    wait_bytes(recv_d.at[2, pl.ds(0, ROWMATES - 1)], d_recv.at[2])
    last_pieces[...] = recv_d[2]
    statistics(2)

    for k in range(SLOTS):
        wait_bytes(send_a.at[k, pl.ds(0, ROWMATES - 1)], a_send.at[k])
        wait_bytes(send_d.at[k, pl.ds(0, ROWMATES - 1)], d_send.at[k])

        @pl.when(worker(k, plane) != c)
        def _():
            wait_bytes(send_b.at[k], b_send.at[k])

        @pl.when(worker(k, plane) == c)
        def _():
            wait_bytes(send_b.at[k, pl.ds(0, PLANES - 1)], b_send.at[k])

    @pl.when(own_slot < SLOTS)
    def _():
        wait_bytes(g.at[pl.ds(0, PLANES * MEMBERS - 1)], c_send)
        for i in range(2):
            wait_bytes(outer_recv.at[0], outer_sent.at[i])
        wait_bytes(outer_relay_0, outer_sent.at[2])
        wait_bytes(outer_relay_1, outer_sent.at[3])

    @pl.when(right_slot < SLOTS)
    def _():
        wait_bytes(full.at[:, 0], root_send.at[0])
        wait_bytes(root_relay_0, root_send.at[4])
        wait_bytes(outer_relay_1, outer_sent.at[5])

    @pl.when(left_slot < SLOTS)
    def _():
        wait_bytes(full.at[:, 0], root_send.at[1])
        wait_bytes(root_relay_1, root_send.at[5])
        wait_bytes(outer_relay_0, outer_sent.at[4])

    @pl.when(far_slot < SLOTS)
    def _():
        wait_bytes(root_relay_0, root_send.at[2])
        wait_bytes(root_relay_1, root_send.at[3])


def last_kernel(
    new_left, new_right, total, last_spread, last_pieces, left_out, right_out, precond_out, by_row, precond, sem
):
    copies = [
        pltpu.make_async_copy(source.at[k], result.at[k], sem.at[3 * i + k])
        for i, (source, result) in enumerate(((new_left, left_out), (new_right, right_out)))
        for k in range(SLOTS)
    ]
    for copy in copies:
        copy.start()
    blocks = total[...] + dot(last_spread[...], side_by_side(last_pieces[...]))
    for i in range(4):
        by_row[pl.ds(i, 384, stride=4), :] = blocks[:, 128 * i : 128 * i + 128]
    precond[...] = by_row[...].astype(BF16)
    copies.append(pltpu.make_async_copy(precond, precond_out, sem.at[6]))
    copies[-1].start()
    for copy in copies:
        copy.wait()


def local(grads, owner, left_stat, right_stat, left_root, right_root):
    any_space = pl.BlockSpec(memory_space=pl.ANY)
    vmem = pl.BlockSpec(memory_space=pltpu.VMEM)
    dma = pltpu.SemaphoreType.DMA
    results = pl.pallas_call(
        kernel,
        out_shape=(
            pltpu.VMEM((3, 128, 512), F32),
            pltpu.VMEM((3, 128, 512), F32),
            pltpu.VMEM((384, 512), F32),
            pltpu.VMEM((384, 128), BF16),
            pltpu.VMEM((16, 32, 128), BF16),
        ),
        in_specs=[any_space] * 6,
        out_specs=(vmem,) * 5,
        scratch_shapes=[
            pltpu.VMEM((1536, 128), BF16),
            pltpu.VMEM((3, 128), jnp.int32),
            pltpu.VMEM((3, 128, 512), F32),
            pltpu.VMEM((3, 128, 512), F32),
            pltpu.VMEM((8, 384), F32),
            pltpu.VMEM((1536, 128), F32),
            pltpu.VMEM((384, 512), BF16),
            pltpu.VMEM((384, 384), BF16),
            pltpu.VMEM((512, 128), F32),
            pltpu.VMEM((3, 16, 32, 128), BF16),
            pltpu.VMEM((3, 16, 32, 128), BF16),
            pltpu.VMEM((3, 8, 64, 128), BF16),
            pltpu.VMEM((32, 64, 128), BF16),
            pltpu.VMEM((2, 3, 128, 512), BF16),
            pltpu.VMEM((2, 4, 128, 512), BF16),
            pltpu.VMEM((2, VIA_RIGHT, 512), BF16),
            pltpu.VMEM((2, 128 - VIA_RIGHT, 512), BF16),
            pltpu.VMEM((512, 512), F32),
            pltpu.VMEM((4, 8, 64, 128), BF16),
            pltpu.VMEM((3, 8, 64, 128), BF16),
            pltpu.VMEM((3, 16, 32, 128), BF16),
            pltpu.VMEM((3, 16, 32, 128), BF16),
            pltpu.VMEM((2, 4, 128, 512), BF16),
            pltpu.VMEM((3, 2, 128, 512), BF16),
            pltpu.VMEM((2, VIA_RIGHT, 512), BF16),
            pltpu.VMEM((2, 128 - VIA_RIGHT, 512), BF16),
            dma((6,)),
            dma((3,)), dma((3,)),
            dma((3,)), dma,
            dma, dma((3, 2)),
            dma((3,)), dma((3,)),
            dma((6,)), dma, dma((2,)),
            dma((6,)), dma((3,)), dma((2,)),
            pltpu.SemaphoreType.REGULAR,
        ],
        compiler_params=pltpu.CompilerParams(
            collective_id=0, has_side_effects=True, vmem_limit_bytes=58 * 1024 * 1024
        ),
        cost_estimate=pl.CostEstimate(flops=4_000_000_000, bytes_accessed=6_000_000, transcendentals=0),
    )(grads.reshape(1536, 128), owner.reshape(3, 128), left_stat, right_stat, left_root, right_root)
    new_left, new_right, precond = pl.pallas_call(
        last_kernel,
        out_shape=(
            jax.ShapeDtypeStruct((3, 128, 512), F32),
            jax.ShapeDtypeStruct((3, 128, 512), F32),
            jax.ShapeDtypeStruct((1536, 128), BF16),
        ),
        in_specs=[vmem] * 5,
        out_specs=(any_space,) * 3,
        scratch_shapes=[pltpu.VMEM((1536, 128), F32), pltpu.VMEM((1536, 128), BF16), dma((7,))],
        compiler_params=pltpu.CompilerParams(vmem_limit_bytes=4 * 1024 * 1024),
        cost_estimate=pl.CostEstimate(flops=0, bytes_accessed=4_000_000, transcendentals=0),
    )(*results)
    return new_left, new_right, precond.reshape(384, 4, 128)


def solution(mesh):
    in_specs = (
        P(None, "dp", "mp"),
        P(),
        P("dp", "mp", None),
        P("dp", "mp", None),
        P("dp", "mp", None),
        P("dp", "mp", None),
    )
    out_specs = (P("dp", "mp", None), P("dp", "mp", None), P(None, "dp", "mp"))
    return jax.shard_map(local, mesh=mesh, in_specs=in_specs, out_specs=out_specs, check_vma=False)
```

```python
import jax
import jax.numpy as jnp
from jax import lax
from jax.experimental import pallas as pl
from jax.experimental.pallas import tpu as pltpu
from jax.sharding import PartitionSpec as P

DECAY = 0.9
EPSILON = 1e-06
MESH = pl.DeviceIdType.MESH
F32 = jnp.float32
BF16 = jnp.bfloat16
SLOTS = 3
HALVES = 2
PLANES = 8
ROWMATES = 16
MEMBERS = 4
VIA_RIGHT = 32


def one_hot(condition):
    return jnp.where(condition, 1.0, 0.0).astype(BF16)


def iota(shape, dim):
    return lax.broadcasted_iota(jnp.int32, shape, dim)


def dot(a, b, contract=((1,), (0,))):
    return lax.dot_general(a, b, (contract, ((), ())), preferred_element_type=F32)


def across(row, tall):
    return jnp.concatenate(
        [one_hot(tall == row[:, 128 * t : 128 * t + 128]) for t in range(row.shape[1] // 128)], axis=1
    )


def sorted_block(index):
    slot, rowmate, plane = index >> 7, (index >> 3) & 15, index & 7
    return (plane * ROWMATES + rowmate) * SLOTS + slot


def side_by_side(pieces):
    rows = pieces.astype(F32).reshape(ROWMATES, 4, PLANES, 128)
    return jnp.concatenate([rows[:, i].reshape(128, 128) for i in range(4)], axis=1).astype(BF16)


def kernel(
    grads_in, owner_in, left_stat, right_stat, left_root, right_root,
    new_left, new_right, total, last_spread, last_pieces,
    grads, owner, l_stat, r_stat, target, by_row, blocks, spread, stage,
    send_a, recv_a, send_b, g, roots, full, root_relay_0, root_relay_1, p, send_c, recv_c, send_d, recv_d,
    outer_send, outer_recv, outer_relay_0, outer_relay_1,
    local_sem, a_send, a_recv, b_send, b_recv, c_send, c_recv, d_send, d_recv,
    root_send, root_recv, root_relay_recv, outer_sent, outer_arrived, outer_relay_recv, members_in,
):
    d = lax.axis_index("dp")
    c = lax.axis_index("mp")
    plane = d // ROWMATES
    mate = d % ROWMATES
    right = lax.rem(c + 1, MEMBERS)
    left = lax.rem(c + MEMBERS - 1, MEMBERS)
    far = lax.rem(c + 2, MEMBERS)
    to_right, to_left = (d, right), (d, left)

    twice = 2 * lax.rem(d, 2)
    shift = lax.rem(twice + plane, MEMBERS)
    own_slot, right_slot, far_slot, left_slot = [lax.rem(c + i + MEMBERS - shift, MEMBERS) for i in range(MEMBERS)]

    def worker(k, owner_plane):
        return lax.rem(k + twice + owner_plane, MEMBERS)

    def far_first(j, count):
        return count // 2 + (j // 2) * (2 * (j % 2) - 1)

    def mate_at(j):
        other = lax.rem(mate + far_first(j, ROWMATES), ROWMATES)
        return other, plane * ROWMATES + other

    def plane_at(j):
        other = lax.rem(plane + far_first(j, PLANES), PLANES)
        return other, other * ROWMATES + mate

    def remote(src, dst, send, recv, device):
        return pltpu.make_async_remote_copy(
            src_ref=src, dst_ref=dst, send_sem=send, recv_sem=recv, device_id=device, device_id_type=MESH
        )

    def wait_bytes(ref, sem):
        pltpu.make_async_copy(ref, ref, sem).wait()

    def aligned(start, size):
        return pl.ds(pl.multiple_of(start, size), size)

    own = [
        pltpu.make_async_copy(owner_in, owner, local_sem.at[5]),
        pltpu.make_async_copy(grads_in, grads, local_sem.at[0]),
        pltpu.make_async_copy(left_root, roots.at[0], local_sem.at[1]),
        pltpu.make_async_copy(right_root, roots.at[1], local_sem.at[2]),
        pltpu.make_async_copy(left_stat, l_stat, local_sem.at[3]),
        pltpu.make_async_copy(right_stat, r_stat, local_sem.at[4]),
    ]
    for copy in own[:2]:
        copy.start()

    barrier = pltpu.get_barrier_semaphore()

    @pl.loop(1, ROWMATES, unroll=True)
    def _(j):
        pl.semaphore_signal(barrier, inc=1, device_id=(mate_at(j)[1], c), device_id_type=MESH)

    @pl.loop(1, MEMBERS, unroll=True)
    def _(j):
        pl.semaphore_signal(barrier, inc=1, device_id=(d, lax.rem(c + j, MEMBERS)), device_id_type=MESH)

    @pl.loop(1, PLANES, unroll=True)
    def _(j):
        pl.semaphore_signal(barrier, inc=1, device_id=(plane_at(j)[1], c), device_id_type=MESH)

    for copy in own[2:]:
        copy.start()

    def tell_column():
        @pl.loop(1, PLANES, unroll=True)
        def _(j):
            pl.semaphore_signal(members_in, inc=1, device_id=(plane_at(j)[1], c), device_id_type=MESH)

    top, bottom = pl.ds(0, VIA_RIGHT), pl.ds(VIA_RIGHT, 128 - VIA_RIGHT)

    def start_roots():
        @pl.when(far_slot < SLOTS)
        def _():
            remote(
                roots.at[:, far_slot, top], root_relay_0, root_send.at[2], root_relay_recv.at[0], to_right
            ).start()
            remote(
                roots.at[:, far_slot, bottom], root_relay_1, root_send.at[3], root_relay_recv.at[1], to_left
            ).start()

        @pl.when(right_slot < SLOTS)
        def _():
            remote(roots.at[:, right_slot], full.at[:, c], root_send.at[0], root_recv, to_right).start()

        @pl.when(left_slot < SLOTS)
        def _():
            remote(roots.at[:, left_slot], full.at[:, c], root_send.at[1], root_recv, to_left).start()

        @pl.when(own_slot < SLOTS)
        def _():
            full[:, c] = roots[:, own_slot]

    def pass_roots():
        @pl.when(right_slot < SLOTS)
        def _():
            wait_bytes(root_relay_0, root_relay_recv.at[0])
            remote(root_relay_0, full.at[:, left, top], root_send.at[4], root_recv, to_right).start()

        @pl.when(left_slot < SLOTS)
        def _():
            wait_bytes(root_relay_1, root_relay_recv.at[1])
            remote(root_relay_1, full.at[:, right, bottom], root_send.at[5], root_recv, to_left).start()

    def make_a(k):
        wanted = sorted_block(iota((128, 128), 0) + 128 * k).astype(F32)
        moved = dot(across(target[0:1, :], wanted), blocks[...])
        rows = [moved[:, 128 * i : 128 * i + 128].reshape(ROWMATES, 1, PLANES, 128) for i in range(4)]
        send_a[k] = jnp.concatenate(rows, axis=1).reshape(ROWMATES, 32, 128).astype(BF16)

    def start_a(k):
        @pl.loop(1, ROWMATES, unroll=True)
        def _(j):
            other, device = mate_at(j)
            remote(send_a.at[k, other], recv_a.at[k, mate], a_send.at[k], a_recv.at[k], (device, c)).start()

        recv_a[k, mate] = send_a[k, mate]

    def start_b(k):
        wait_bytes(recv_a.at[k, pl.ds(0, ROWMATES - 1)], a_recv.at[k])
        stage[...] = recv_a[k].reshape(512, 128).astype(F32)
        for i in range(PLANES):
            send_b[k, i] = stage[pl.ds(i, 64, stride=PLANES), :].astype(BF16)
        member = worker(k, plane)
        place = c * PLANES + plane

        @pl.loop(1, PLANES, unroll=True)
        def _(j):
            other, device = plane_at(j)
            remote(send_b.at[k, other], g.at[place], b_send.at[k], b_recv, (device, worker(k, other))).start()

        @pl.when(member != c)
        def _():
            remote(send_b.at[k, plane], g.at[place], b_send.at[k], b_recv, (d, member)).start()

        @pl.when(member == c)
        def _():
            g[place] = send_b[k, plane]

    def gradient():
        parts = [g[pl.ds(PLANES * j, PLANES)].reshape(512, 128) for j in range(MEMBERS)]
        return jnp.concatenate(parts, axis=1)

    def work():
        wait_bytes(full.at[:, pl.ds(0, MEMBERS - 1)], root_recv)
        wait_bytes(g.at[pl.ds(0, PLANES * MEMBERS - 1)], b_recv)
        wide = gradient()
        half_way = dot(wide, full[1].reshape(512, 512)).astype(BF16)
        p[...] = dot(full[0].reshape(512, 512), half_way)
        grad_squares = jnp.zeros((1, 512), F32)
        product_squares = jnp.zeros((1, 512), F32)
        for i in range(4):
            part = wide[128 * i : 128 * i + 128].astype(F32)
            grad_squares = grad_squares + jnp.sum(part * part, axis=0, keepdims=True)
            part = p[pl.ds(128 * i, 128), :]
            product_squares = product_squares + jnp.sum(part * part, axis=0, keepdims=True)
        grad_squares = jnp.sum(grad_squares, axis=1, keepdims=True)
        product_squares = jnp.sum(product_squares, axis=1, keepdims=True)
        scale = jnp.sqrt(grad_squares / (product_squares + EPSILON))
        for j in range(MEMBERS):
            send_c[j] = (p[:, 128 * j : 128 * j + 128] * scale).astype(BF16).reshape(PLANES, 64, 128)

        for half in range(HALVES):
            rows = pl.ds(32 * half, 32)

            def send(member, other):
                remote(
                    send_c.at[member, other, rows], recv_c.at[own_slot, plane, rows],
                    c_send, c_recv.at[own_slot, half], (other * ROWMATES + mate, member),
                ).start()

            @pl.loop(0, (PLANES - 1) * MEMBERS, unroll=True)
            def _(j):
                send(lax.rem(c + 2 + j % MEMBERS, MEMBERS), plane_at(j // MEMBERS + 1)[0])

            @pl.loop(1, MEMBERS, unroll=True)
            def _(j):
                send(lax.rem(c + j, MEMBERS), plane)

        recv_c[own_slot, plane] = send_c[c, plane]

    def outer_products():
        wide = gradient()
        outer_send[0] = dot(wide, wide, ((1,), (1,))).astype(BF16).reshape(MEMBERS, 128, 512)
        outer_send[1] = dot(wide, wide, ((0,), (0,))).astype(BF16).reshape(MEMBERS, 128, 512)
        remote(
            outer_send.at[:, far, top], outer_relay_0, outer_sent.at[2], outer_relay_recv.at[0], to_right
        ).start()
        remote(
            outer_send.at[:, far, bottom], outer_relay_1, outer_sent.at[3], outer_relay_recv.at[1], to_left
        ).start()
        for number, (member, device) in enumerate(((right, to_right), (left, to_left))):
            remote(
                outer_send.at[:, member], outer_recv.at[own_slot],
                outer_sent.at[number], outer_arrived.at[own_slot], device,
            ).start()
        outer_recv[own_slot] = outer_send[:, c]

    def pass_outer(k):
        @pl.when(left_slot == k)
        def _():
            wait_bytes(outer_relay_0, outer_relay_recv.at[0])
            remote(
                outer_relay_0, outer_recv.at[k, :, top],
                outer_sent.at[4], outer_arrived.at[k], to_right,
            ).start()

        @pl.when(right_slot == k)
        def _():
            wait_bytes(outer_relay_1, outer_relay_recv.at[1])
            remote(
                outer_relay_1, outer_recv.at[k, :, bottom],
                outer_sent.at[5], outer_arrived.at[k], to_left,
            ).start()

    def statistics(k):
        @pl.when(worker(k, plane) != c)
        def _():
            wait_bytes(outer_recv.at[k], outer_arrived.at[k])

        new_left[k] = DECAY * l_stat[k] + (1.0 - DECAY) / 512 * outer_recv[k, 0].astype(F32)
        new_right[k] = DECAY * r_stat[k] + (1.0 - DECAY) / 512 * outer_recv[k, 1].astype(F32)

    def start_d(k):
        for half in range(HALVES):
            rows = pl.ds(32 * half, 32)

            @pl.when(worker(k, plane) != c)
            def _():
                wait_bytes(recv_c.at[k, :, rows], c_recv.at[k, half])

            @pl.when(worker(k, plane) == c)
            def _():
                wait_bytes(recv_c.at[k, pl.ds(0, PLANES - 1), rows], c_recv.at[k, half])

            for i in range(PLANES):
                stage[pl.ds(i, 32, stride=PLANES), :] = recv_c[k, i, rows].astype(F32)
            send_d[k, pl.ds(8 * half, 8)] = stage[pl.ds(0, 256), :].astype(BF16).reshape(8, 32, 128)

            @pl.loop(0, 8, unroll=True)
            def _(j):
                other = 8 * half + lax.rem(mate + 4 + j, 8)

                @pl.when(other != mate)
                def _():
                    device = (plane * ROWMATES + other, c)
                    remote(send_d.at[k, other], recv_d.at[k, mate], d_send.at[k], d_recv.at[k], device).start()

        recv_d[k, mate] = send_d[k, mate]

    def finish(k):
        wait_bytes(recv_d.at[k, pl.ds(0, ROWMATES - 1)], d_recv.at[k])
        part = dot(spread[:, 128 * k : 128 * k + 128], side_by_side(recv_d[k]))
        total[...] = part if k == 0 else part + total[...]

    own[0].wait()
    owned = jnp.concatenate([one_hot(owner[i : i + 1, :] == iota((128, 128), 0)) for i in range(3)], axis=1)
    earlier = iota((128, 384), 0).astype(F32) * SLOTS
    for i in range(3):
        earlier += dot(
            owned[:, 128 * i : 128 * i + 128], one_hot(iota((128, 384), 0) + 128 * i < iota((128, 384), 1))
        )
    number = jnp.sum(owned.astype(F32) * earlier, axis=0, keepdims=True)
    target[...] = jnp.broadcast_to(number, (8, 384))

    own[1].wait()
    by_row[...] = grads[...].astype(F32)
    for i in range(4):
        blocks[:, 128 * i : 128 * i + 128] = by_row[pl.ds(i, 384, stride=4), :].astype(BF16)
    make_a(0)
    own[2].wait()
    own[3].wait()
    pl.semaphore_wait(barrier, ROWMATES + MEMBERS + PLANES - 3)
    start_roots()
    start_a(0)
    tell_column()
    for k in (1, 2):
        make_a(k)
        start_a(k)
    column = jnp.transpose(jnp.broadcast_to(target[0:1, :], (128, 384)))
    spread[...] = across(sorted_block(iota((1, 384), 1)).astype(F32), column)

    pass_roots()
    pl.semaphore_wait(members_in, PLANES - 1)
    start_b(0)
    start_b(1)
    start_b(2)
    for copy in own[4:]:
        copy.wait()
    pl.when(own_slot < SLOTS)(work)
    pl.when(own_slot < SLOTS)(outer_products)
    for k in range(SLOTS):
        start_d(k)
        pass_outer(k)
    finish(0)
    finish(1)
    statistics(0)
    statistics(1)
    last_spread[...] = spread[:, 256:384]
    wait_bytes(recv_d.at[2, pl.ds(0, ROWMATES - 1)], d_recv.at[2])
    last_pieces[...] = recv_d[2]
    statistics(2)

    for k in range(SLOTS):
        wait_bytes(send_a.at[k, pl.ds(0, ROWMATES - 1)], a_send.at[k])
        wait_bytes(send_d.at[k, pl.ds(0, ROWMATES - 1)], d_send.at[k])

        @pl.when(worker(k, plane) != c)
        def _():
            wait_bytes(send_b.at[k], b_send.at[k])

        @pl.when(worker(k, plane) == c)
        def _():
            wait_bytes(send_b.at[k, pl.ds(0, PLANES - 1)], b_send.at[k])

    @pl.when(own_slot < SLOTS)
    def _():
        wait_bytes(g.at[pl.ds(0, PLANES * MEMBERS - 1)], c_send)
        for i in range(2):
            wait_bytes(outer_recv.at[0], outer_sent.at[i])
        wait_bytes(outer_relay_0, outer_sent.at[2])
        wait_bytes(outer_relay_1, outer_sent.at[3])

    @pl.when(right_slot < SLOTS)
    def _():
        wait_bytes(full.at[:, 0], root_send.at[0])
        wait_bytes(root_relay_0, root_send.at[4])
        wait_bytes(outer_relay_1, outer_sent.at[5])

    @pl.when(left_slot < SLOTS)
    def _():
        wait_bytes(full.at[:, 0], root_send.at[1])
        wait_bytes(root_relay_1, root_send.at[5])
        wait_bytes(outer_relay_0, outer_sent.at[4])

    @pl.when(far_slot < SLOTS)
    def _():
        wait_bytes(root_relay_0, root_send.at[2])
        wait_bytes(root_relay_1, root_send.at[3])


def last_kernel(
    new_left, new_right, total, last_spread, last_pieces, left_out, right_out, precond_out, by_row, precond, sem
):
    copies = [
        pltpu.make_async_copy(source.at[k], result.at[k], sem.at[3 * i + k])
        for i, (source, result) in enumerate(((new_left, left_out), (new_right, right_out)))
        for k in range(SLOTS)
    ]
    for copy in copies:
        copy.start()
    blocks = total[...] + dot(last_spread[...], side_by_side(last_pieces[...]))
    for i in range(4):
        by_row[pl.ds(i, 384, stride=4), :] = blocks[:, 128 * i : 128 * i + 128]
    precond[...] = by_row[...].astype(BF16)
    copies.append(pltpu.make_async_copy(precond, precond_out, sem.at[6]))
    copies[-1].start()
    for copy in copies:
        copy.wait()


def local(grads, owner, left_stat, right_stat, left_root, right_root):
    any_space = pl.BlockSpec(memory_space=pl.ANY)
    vmem = pl.BlockSpec(memory_space=pltpu.VMEM)
    dma = pltpu.SemaphoreType.DMA
    results = pl.pallas_call(
        kernel,
        out_shape=(
            pltpu.VMEM((3, 128, 512), F32),
            pltpu.VMEM((3, 128, 512), F32),
            pltpu.VMEM((384, 512), F32),
            pltpu.VMEM((384, 128), BF16),
            pltpu.VMEM((16, 32, 128), BF16),
        ),
        in_specs=[any_space] * 6,
        out_specs=(vmem,) * 5,
        scratch_shapes=[
            pltpu.VMEM((1536, 128), BF16),
            pltpu.VMEM((3, 128), jnp.int32),
            pltpu.VMEM((3, 128, 512), F32),
            pltpu.VMEM((3, 128, 512), F32),
            pltpu.VMEM((8, 384), F32),
            pltpu.VMEM((1536, 128), F32),
            pltpu.VMEM((384, 512), BF16),
            pltpu.VMEM((384, 384), BF16),
            pltpu.VMEM((512, 128), F32),
            pltpu.VMEM((3, 16, 32, 128), BF16),
            pltpu.VMEM((3, 16, 32, 128), BF16),
            pltpu.VMEM((3, 8, 64, 128), BF16),
            pltpu.VMEM((32, 64, 128), BF16),
            pltpu.VMEM((2, 3, 128, 512), BF16),
            pltpu.VMEM((2, 4, 128, 512), BF16),
            pltpu.VMEM((2, VIA_RIGHT, 512), BF16),
            pltpu.VMEM((2, 128 - VIA_RIGHT, 512), BF16),
            pltpu.VMEM((512, 512), F32),
            pltpu.VMEM((4, 8, 64, 128), BF16),
            pltpu.VMEM((3, 8, 64, 128), BF16),
            pltpu.VMEM((3, 16, 32, 128), BF16),
            pltpu.VMEM((3, 16, 32, 128), BF16),
            pltpu.VMEM((2, 4, 128, 512), BF16),
            pltpu.VMEM((3, 2, 128, 512), BF16),
            pltpu.VMEM((2, VIA_RIGHT, 512), BF16),
            pltpu.VMEM((2, 128 - VIA_RIGHT, 512), BF16),
            dma((6,)),
            dma((3,)), dma((3,)),
            dma((3,)), dma,
            dma, dma((3, 2)),
            dma((3,)), dma((3,)),
            dma((6,)), dma, dma((2,)),
            dma((6,)), dma((3,)), dma((2,)),
            pltpu.SemaphoreType.REGULAR,
        ],
        compiler_params=pltpu.CompilerParams(
            collective_id=0, has_side_effects=True, vmem_limit_bytes=58 * 1024 * 1024
        ),
        cost_estimate=pl.CostEstimate(flops=4_000_000_000, bytes_accessed=6_000_000, transcendentals=0),
    )(grads.reshape(1536, 128), owner.reshape(3, 128), left_stat, right_stat, left_root, right_root)
    new_left, new_right, precond = pl.pallas_call(
        last_kernel,
        out_shape=(
            jax.ShapeDtypeStruct((3, 128, 512), F32),
            jax.ShapeDtypeStruct((3, 128, 512), F32),
            jax.ShapeDtypeStruct((1536, 128), BF16),
        ),
        in_specs=[vmem] * 5,
        out_specs=(any_space,) * 3,
        scratch_shapes=[pltpu.VMEM((1536, 128), F32), pltpu.VMEM((1536, 128), BF16), dma((7,))],
        compiler_params=pltpu.CompilerParams(vmem_limit_bytes=4 * 1024 * 1024),
        cost_estimate=pl.CostEstimate(flops=0, bytes_accessed=4_000_000, transcendentals=0),
    )(*results)
    return new_left, new_right, precond.reshape(384, 4, 128)


def solution(mesh):
    in_specs = (
        P(None, "dp", "mp"),
        P(),
        P("dp", "mp", None),
        P("dp", "mp", None),
        P("dp", "mp", None),
        P("dp", "mp", None),
    )
    out_specs = (P("dp", "mp", None), P("dp", "mp", None), P(None, "dp", "mp"))
    return jax.shard_map(local, mesh=mesh, in_specs=in_specs, out_specs=out_specs, check_vma=False)
```

```python
import jax
import jax.numpy as jnp
from jax import lax
from jax.experimental import pallas as pl
from jax.experimental.pallas import tpu as pltpu
from jax.sharding import PartitionSpec as P

DECAY = 0.9
EPSILON = 1e-06
MESH = pl.DeviceIdType.MESH
F32 = jnp.float32
BF16 = jnp.bfloat16
SLOTS = 3
HALVES = 2
PLANES = 8
ROWMATES = 16
MEMBERS = 4
VIA_RIGHT = 64


def one_hot(condition):
    return jnp.where(condition, 1.0, 0.0).astype(BF16)


def iota(shape, dim):
    return lax.broadcasted_iota(jnp.int32, shape, dim)


def dot(a, b, contract=((1,), (0,))):
    return lax.dot_general(a, b, (contract, ((), ())), preferred_element_type=F32)


def across(row, tall):
    return jnp.concatenate(
        [one_hot(tall == row[:, 128 * t : 128 * t + 128]) for t in range(row.shape[1] // 128)], axis=1
    )


def sorted_block(index):
    slot, rowmate, plane = index >> 7, (index >> 3) & 15, index & 7
    return (plane * ROWMATES + rowmate) * SLOTS + slot


def side_by_side(pieces):
    rows = pieces.astype(F32).reshape(ROWMATES, 4, PLANES, 128)
    return jnp.concatenate([rows[:, i].reshape(128, 128) for i in range(4)], axis=1).astype(BF16)


def kernel(
    grads_in, owner_in, left_stat, right_stat, left_root, right_root,
    new_left, new_right, total, last_spread, last_pieces,
    grads, owner, l_stat, r_stat, target, by_row, blocks, spread, stage,
    send_a, recv_a, send_b, g, roots, full, root_relay_0, root_relay_1, p, send_c, recv_c, send_d, recv_d,
    outer_send, outer_recv, outer_relay_0, outer_relay_1,
    local_sem, a_send, a_recv, b_send, b_recv, c_send, c_recv, d_send, d_recv,
    root_send, root_recv, root_relay_recv, outer_sent, outer_arrived, outer_relay_recv, members_in,
):
    d = lax.axis_index("dp")
    c = lax.axis_index("mp")
    plane = d // ROWMATES
    mate = d % ROWMATES
    right = lax.rem(c + 1, MEMBERS)
    left = lax.rem(c + MEMBERS - 1, MEMBERS)
    far = lax.rem(c + 2, MEMBERS)
    to_right, to_left = (d, right), (d, left)

    twice = 2 * lax.rem(d, 2)
    shift = lax.rem(twice + plane, MEMBERS)
    own_slot, right_slot, far_slot, left_slot = [lax.rem(c + i + MEMBERS - shift, MEMBERS) for i in range(MEMBERS)]

    def worker(k, owner_plane):
        return lax.rem(k + twice + owner_plane, MEMBERS)

    def far_first(j, count):
        return count // 2 + (j // 2) * (2 * (j % 2) - 1)

    def mate_at(j):
        other = lax.rem(mate + far_first(j, ROWMATES), ROWMATES)
        return other, plane * ROWMATES + other

    def plane_at(j):
        other = lax.rem(plane + far_first(j, PLANES), PLANES)
        return other, other * ROWMATES + mate

    def remote(src, dst, send, recv, device):
        return pltpu.make_async_remote_copy(
            src_ref=src, dst_ref=dst, send_sem=send, recv_sem=recv, device_id=device, device_id_type=MESH
        )

    def wait_bytes(ref, sem):
        pltpu.make_async_copy(ref, ref, sem).wait()

    def aligned(start, size):
        return pl.ds(pl.multiple_of(start, size), size)

    own = [
        pltpu.make_async_copy(owner_in, owner, local_sem.at[5]),
        pltpu.make_async_copy(grads_in, grads, local_sem.at[0]),
        pltpu.make_async_copy(left_root, roots.at[0], local_sem.at[1]),
        pltpu.make_async_copy(right_root, roots.at[1], local_sem.at[2]),
        pltpu.make_async_copy(left_stat, l_stat, local_sem.at[3]),
        pltpu.make_async_copy(right_stat, r_stat, local_sem.at[4]),
    ]
    for copy in own[:2]:
        copy.start()

    barrier = pltpu.get_barrier_semaphore()

    @pl.loop(1, ROWMATES, unroll=True)
    def _(j):
        pl.semaphore_signal(barrier, inc=1, device_id=(mate_at(j)[1], c), device_id_type=MESH)

    @pl.loop(1, MEMBERS, unroll=True)
    def _(j):
        pl.semaphore_signal(barrier, inc=1, device_id=(d, lax.rem(c + j, MEMBERS)), device_id_type=MESH)

    @pl.loop(1, PLANES, unroll=True)
    def _(j):
        pl.semaphore_signal(barrier, inc=1, device_id=(plane_at(j)[1], c), device_id_type=MESH)

    for copy in own[2:]:
        copy.start()

    def tell_column():
        @pl.loop(1, PLANES, unroll=True)
        def _(j):
            pl.semaphore_signal(members_in, inc=1, device_id=(plane_at(j)[1], c), device_id_type=MESH)

    top, bottom = pl.ds(0, VIA_RIGHT), pl.ds(VIA_RIGHT, 128 - VIA_RIGHT)

    def start_roots(k):
        @pl.when(far_slot == k)
        def _():
            remote(
                roots.at[:, k, top], root_relay_0, root_send.at[2], root_relay_recv.at[0], to_right
            ).start()
            remote(
                roots.at[:, k, bottom], root_relay_1, root_send.at[3], root_relay_recv.at[1], to_left
            ).start()

        @pl.when(right_slot == k)
        def _():
            remote(roots.at[:, k], full.at[:, c], root_send.at[0], root_recv, to_right).start()

        @pl.when(left_slot == k)
        def _():
            remote(roots.at[:, k], full.at[:, c], root_send.at[1], root_recv, to_left).start()

        @pl.when(own_slot == k)
        def _():
            full[:, c] = roots[:, k]

    def pass_roots(k):
        @pl.when(right_slot == k)
        def _():
            wait_bytes(root_relay_0, root_relay_recv.at[0])
            remote(root_relay_0, full.at[:, left, top], root_send.at[4], root_recv, to_right).start()

        @pl.when(left_slot == k)
        def _():
            wait_bytes(root_relay_1, root_relay_recv.at[1])
            remote(root_relay_1, full.at[:, right, bottom], root_send.at[5], root_recv, to_left).start()

    def make_a(k):
        wanted = sorted_block(iota((128, 128), 0) + 128 * k).astype(F32)
        moved = dot(across(target[0:1, :], wanted), blocks[...])
        rows = [moved[:, 128 * i : 128 * i + 128].reshape(ROWMATES, 1, PLANES, 128) for i in range(4)]
        send_a[k] = jnp.concatenate(rows, axis=1).reshape(ROWMATES, 32, 128).astype(BF16)

    def start_a(k):
        @pl.loop(1, ROWMATES, unroll=True)
        def _(j):
            other, device = mate_at(j)
            remote(send_a.at[k, other], recv_a.at[k, mate], a_send.at[k], a_recv.at[k], (device, c)).start()

        recv_a[k, mate] = send_a[k, mate]

    def start_b(k):
        wait_bytes(recv_a.at[k, pl.ds(0, ROWMATES - 1)], a_recv.at[k])
        stage[...] = recv_a[k].reshape(512, 128).astype(F32)
        for i in range(PLANES):
            send_b[k, i] = stage[pl.ds(i, 64, stride=PLANES), :].astype(BF16)
        member = worker(k, plane)
        place = c * PLANES + plane

        @pl.loop(1, PLANES, unroll=True)
        def _(j):
            other, device = plane_at(j)
            remote(send_b.at[k, other], g.at[place], b_send.at[k], b_recv, (device, worker(k, other))).start()

        @pl.when(member != c)
        def _():
            remote(send_b.at[k, plane], g.at[place], b_send.at[k], b_recv, (d, member)).start()

        @pl.when(member == c)
        def _():
            g[place] = send_b[k, plane]

    def gradient():
        parts = [g[pl.ds(PLANES * j, PLANES)].reshape(512, 128) for j in range(MEMBERS)]
        return jnp.concatenate(parts, axis=1)

    def work():
        wait_bytes(full.at[:, pl.ds(0, MEMBERS - 1)], root_recv)
        wait_bytes(g.at[pl.ds(0, PLANES * MEMBERS - 1)], b_recv)
        wide = gradient()
        half_way = dot(wide, full[1].reshape(512, 512)).astype(BF16)
        p[...] = dot(full[0].reshape(512, 512), half_way)
        grad_squares = jnp.zeros((1, 512), F32)
        product_squares = jnp.zeros((1, 512), F32)
        for i in range(4):
            part = wide[128 * i : 128 * i + 128].astype(F32)
            grad_squares = grad_squares + jnp.sum(part * part, axis=0, keepdims=True)
            part = p[pl.ds(128 * i, 128), :]
            product_squares = product_squares + jnp.sum(part * part, axis=0, keepdims=True)
        grad_squares = jnp.sum(grad_squares, axis=1, keepdims=True)
        product_squares = jnp.sum(product_squares, axis=1, keepdims=True)
        scale = jnp.sqrt(grad_squares / (product_squares + EPSILON))
        for j in range(MEMBERS):
            send_c[j] = (p[:, 128 * j : 128 * j + 128] * scale).astype(BF16).reshape(PLANES, 64, 128)

        for half in range(HALVES):
            rows = pl.ds(32 * half, 32)

            def send(member, other):
                remote(
                    send_c.at[member, other, rows], recv_c.at[own_slot, plane, rows],
                    c_send, c_recv.at[own_slot, half], (other * ROWMATES + mate, member),
                ).start()

            @pl.loop(0, (PLANES - 1) * MEMBERS, unroll=True)
            def _(j):
                send(lax.rem(c + 2 + j % MEMBERS, MEMBERS), plane_at(j // MEMBERS + 1)[0])

            @pl.loop(1, MEMBERS, unroll=True)
            def _(j):
                send(lax.rem(c + j, MEMBERS), plane)

        recv_c[own_slot, plane] = send_c[c, plane]

    def outer_products():
        wide = gradient()
        outer_send[0] = dot(wide, wide, ((1,), (1,))).astype(BF16).reshape(MEMBERS, 128, 512)
        outer_send[1] = dot(wide, wide, ((0,), (0,))).astype(BF16).reshape(MEMBERS, 128, 512)
        remote(
            outer_send.at[:, far, top], outer_relay_0, outer_sent.at[2], outer_relay_recv.at[0], to_right
        ).start()
        remote(
            outer_send.at[:, far, bottom], outer_relay_1, outer_sent.at[3], outer_relay_recv.at[1], to_left
        ).start()
        for number, (member, device) in enumerate(((right, to_right), (left, to_left))):
            remote(
                outer_send.at[:, member], outer_recv.at[own_slot],
                outer_sent.at[number], outer_arrived.at[own_slot], device,
            ).start()
        outer_recv[own_slot] = outer_send[:, c]

    def pass_outer(k):
        @pl.when(left_slot == k)
        def _():
            wait_bytes(outer_relay_0, outer_relay_recv.at[0])
            remote(
                outer_relay_0, outer_recv.at[k, :, top],
                outer_sent.at[4], outer_arrived.at[k], to_right,
            ).start()

        @pl.when(right_slot == k)
        def _():
            wait_bytes(outer_relay_1, outer_relay_recv.at[1])
            remote(
                outer_relay_1, outer_recv.at[k, :, bottom],
                outer_sent.at[5], outer_arrived.at[k], to_left,
            ).start()

    def statistics(k):
        @pl.when(worker(k, plane) != c)
        def _():
            wait_bytes(outer_recv.at[k], outer_arrived.at[k])

        new_left[k] = DECAY * l_stat[k] + (1.0 - DECAY) / 512 * outer_recv[k, 0].astype(F32)
        new_right[k] = DECAY * r_stat[k] + (1.0 - DECAY) / 512 * outer_recv[k, 1].astype(F32)

    def start_d(k):
        for half in range(HALVES):
            rows = pl.ds(32 * half, 32)

            @pl.when(worker(k, plane) != c)
            def _():
                wait_bytes(recv_c.at[k, :, rows], c_recv.at[k, half])

            @pl.when(worker(k, plane) == c)
            def _():
                wait_bytes(recv_c.at[k, pl.ds(0, PLANES - 1), rows], c_recv.at[k, half])

            for i in range(PLANES):
                stage[pl.ds(i, 32, stride=PLANES), :] = recv_c[k, i, rows].astype(F32)
            send_d[k, pl.ds(8 * half, 8)] = stage[pl.ds(0, 256), :].astype(BF16).reshape(8, 32, 128)

            @pl.loop(0, 8, unroll=True)
            def _(j):
                other = 8 * half + lax.rem(mate + 4 + j, 8)

                @pl.when(other != mate)
                def _():
                    device = (plane * ROWMATES + other, c)
                    remote(send_d.at[k, other], recv_d.at[k, mate], d_send.at[k], d_recv.at[k], device).start()

        recv_d[k, mate] = send_d[k, mate]

    def finish(k):
        wait_bytes(recv_d.at[k, pl.ds(0, ROWMATES - 1)], d_recv.at[k])
        part = dot(spread[:, 128 * k : 128 * k + 128], side_by_side(recv_d[k]))
        total[...] = part if k == 0 else part + total[...]

    own[0].wait()
    owned = jnp.concatenate([one_hot(owner[i : i + 1, :] == iota((128, 128), 0)) for i in range(3)], axis=1)
    earlier = iota((128, 384), 0).astype(F32) * SLOTS
    for i in range(3):
        earlier += dot(
            owned[:, 128 * i : 128 * i + 128], one_hot(iota((128, 384), 0) + 128 * i < iota((128, 384), 1))
        )
    number = jnp.sum(owned.astype(F32) * earlier, axis=0, keepdims=True)
    target[...] = jnp.broadcast_to(number, (8, 384))

    own[1].wait()
    by_row[...] = grads[...].astype(F32)
    for i in range(4):
        blocks[:, 128 * i : 128 * i + 128] = by_row[pl.ds(i, 384, stride=4), :].astype(BF16)
    make_a(0)
    own[2].wait()
    own[3].wait()
    pl.semaphore_wait(barrier, ROWMATES + MEMBERS + PLANES - 3)
    start_roots(0)
    start_a(0)
    tell_column()
    for k in (1, 2):
        start_roots(k)
        make_a(k)
        start_a(k)
    column = jnp.transpose(jnp.broadcast_to(target[0:1, :], (128, 384)))
    spread[...] = across(sorted_block(iota((1, 384), 1)).astype(F32), column)

    pl.semaphore_wait(members_in, PLANES - 1)
    for k in range(SLOTS):
        start_b(k)
        pass_roots(k)
    for copy in own[4:]:
        copy.wait()
    pl.when(own_slot < SLOTS)(work)
    pl.when(own_slot < SLOTS)(outer_products)
    for k in range(SLOTS):
        start_d(k)
        pass_outer(k)
    finish(0)
    finish(1)
    statistics(0)
    statistics(1)
    last_spread[...] = spread[:, 256:384]
    wait_bytes(recv_d.at[2, pl.ds(0, ROWMATES - 1)], d_recv.at[2])
    last_pieces[...] = recv_d[2]
    statistics(2)

    for k in range(SLOTS):
        wait_bytes(send_a.at[k, pl.ds(0, ROWMATES - 1)], a_send.at[k])
        wait_bytes(send_d.at[k, pl.ds(0, ROWMATES - 1)], d_send.at[k])

        @pl.when(worker(k, plane) != c)
        def _():
            wait_bytes(send_b.at[k], b_send.at[k])

        @pl.when(worker(k, plane) == c)
        def _():
            wait_bytes(send_b.at[k, pl.ds(0, PLANES - 1)], b_send.at[k])

    @pl.when(own_slot < SLOTS)
    def _():
        wait_bytes(g.at[pl.ds(0, PLANES * MEMBERS - 1)], c_send)
        for i in range(2):
            wait_bytes(outer_recv.at[0], outer_sent.at[i])
        wait_bytes(outer_relay_0, outer_sent.at[2])
        wait_bytes(outer_relay_1, outer_sent.at[3])

    @pl.when(right_slot < SLOTS)
    def _():
        wait_bytes(full.at[:, 0], root_send.at[0])
        wait_bytes(root_relay_0, root_send.at[4])
        wait_bytes(outer_relay_1, outer_sent.at[5])

    @pl.when(left_slot < SLOTS)
    def _():
        wait_bytes(full.at[:, 0], root_send.at[1])
        wait_bytes(root_relay_1, root_send.at[5])
        wait_bytes(outer_relay_0, outer_sent.at[4])

    @pl.when(far_slot < SLOTS)
    def _():
        wait_bytes(root_relay_0, root_send.at[2])
        wait_bytes(root_relay_1, root_send.at[3])


def last_kernel(
    new_left, new_right, total, last_spread, last_pieces, left_out, right_out, precond_out, by_row, precond, sem
):
    copies = [
        pltpu.make_async_copy(source.at[k], result.at[k], sem.at[3 * i + k])
        for i, (source, result) in enumerate(((new_left, left_out), (new_right, right_out)))
        for k in range(SLOTS)
    ]
    for copy in copies:
        copy.start()
    blocks = total[...] + dot(last_spread[...], side_by_side(last_pieces[...]))
    for i in range(4):
        by_row[pl.ds(i, 384, stride=4), :] = blocks[:, 128 * i : 128 * i + 128]
    precond[...] = by_row[...].astype(BF16)
    copies.append(pltpu.make_async_copy(precond, precond_out, sem.at[6]))
    copies[-1].start()
    for copy in copies:
        copy.wait()


def local(grads, owner, left_stat, right_stat, left_root, right_root):
    any_space = pl.BlockSpec(memory_space=pl.ANY)
    vmem = pl.BlockSpec(memory_space=pltpu.VMEM)
    dma = pltpu.SemaphoreType.DMA
    results = pl.pallas_call(
        kernel,
        out_shape=(
            pltpu.VMEM((3, 128, 512), F32),
            pltpu.VMEM((3, 128, 512), F32),
            pltpu.VMEM((384, 512), F32),
            pltpu.VMEM((384, 128), BF16),
            pltpu.VMEM((16, 32, 128), BF16),
        ),
        in_specs=[any_space] * 6,
        out_specs=(vmem,) * 5,
        scratch_shapes=[
            pltpu.VMEM((1536, 128), BF16),
            pltpu.VMEM((3, 128), jnp.int32),
            pltpu.VMEM((3, 128, 512), F32),
            pltpu.VMEM((3, 128, 512), F32),
            pltpu.VMEM((8, 384), F32),
            pltpu.VMEM((1536, 128), F32),
            pltpu.VMEM((384, 512), BF16),
            pltpu.VMEM((384, 384), BF16),
            pltpu.VMEM((512, 128), F32),
            pltpu.VMEM((3, 16, 32, 128), BF16),
            pltpu.VMEM((3, 16, 32, 128), BF16),
            pltpu.VMEM((3, 8, 64, 128), BF16),
            pltpu.VMEM((32, 64, 128), BF16),
            pltpu.VMEM((2, 3, 128, 512), BF16),
            pltpu.VMEM((2, 4, 128, 512), BF16),
            pltpu.VMEM((2, VIA_RIGHT, 512), BF16),
            pltpu.VMEM((2, 128 - VIA_RIGHT, 512), BF16),
            pltpu.VMEM((512, 512), F32),
            pltpu.VMEM((4, 8, 64, 128), BF16),
            pltpu.VMEM((3, 8, 64, 128), BF16),
            pltpu.VMEM((3, 16, 32, 128), BF16),
            pltpu.VMEM((3, 16, 32, 128), BF16),
            pltpu.VMEM((2, 4, 128, 512), BF16),
            pltpu.VMEM((3, 2, 128, 512), BF16),
            pltpu.VMEM((2, VIA_RIGHT, 512), BF16),
            pltpu.VMEM((2, 128 - VIA_RIGHT, 512), BF16),
            dma((6,)),
            dma((3,)), dma((3,)),
            dma((3,)), dma,
            dma, dma((3, 2)),
            dma((3,)), dma((3,)),
            dma((6,)), dma, dma((2,)),
            dma((6,)), dma((3,)), dma((2,)),
            pltpu.SemaphoreType.REGULAR,
        ],
        compiler_params=pltpu.CompilerParams(
            collective_id=0, has_side_effects=True, vmem_limit_bytes=58 * 1024 * 1024
        ),
        cost_estimate=pl.CostEstimate(flops=4_000_000_000, bytes_accessed=6_000_000, transcendentals=0),
    )(grads.reshape(1536, 128), owner.reshape(3, 128), left_stat, right_stat, left_root, right_root)
    new_left, new_right, precond = pl.pallas_call(
        last_kernel,
        out_shape=(
            jax.ShapeDtypeStruct((3, 128, 512), F32),
            jax.ShapeDtypeStruct((3, 128, 512), F32),
            jax.ShapeDtypeStruct((1536, 128), BF16),
        ),
        in_specs=[vmem] * 5,
        out_specs=(any_space,) * 3,
        scratch_shapes=[pltpu.VMEM((1536, 128), F32), pltpu.VMEM((1536, 128), BF16), dma((7,))],
        compiler_params=pltpu.CompilerParams(vmem_limit_bytes=4 * 1024 * 1024),
        cost_estimate=pl.CostEstimate(flops=0, bytes_accessed=4_000_000, transcendentals=0),
    )(*results)
    return new_left, new_right, precond.reshape(384, 4, 128)


def solution(mesh):
    in_specs = (
        P(None, "dp", "mp"),
        P(),
        P("dp", "mp", None),
        P("dp", "mp", None),
        P("dp", "mp", None),
        P("dp", "mp", None),
    )
    out_specs = (P("dp", "mp", None), P("dp", "mp", None), P(None, "dp", "mp"))
    return jax.shard_map(local, mesh=mesh, in_specs=in_specs, out_specs=out_specs, check_vma=False)
```

```python
import jax
import jax.numpy as jnp
from jax import lax
from jax.experimental import pallas as pl
from jax.experimental.pallas import tpu as pltpu
from jax.sharding import PartitionSpec as P

DECAY = 0.9
EPSILON = 1e-06
MESH = pl.DeviceIdType.MESH
F32 = jnp.float32
BF16 = jnp.bfloat16
SLOTS = 3
HALVES = 2
PLANES = 8
ROWMATES = 16
MEMBERS = 4
VIA_RIGHT = 64


def one_hot(condition):
    return jnp.where(condition, 1.0, 0.0).astype(BF16)


def iota(shape, dim):
    return lax.broadcasted_iota(jnp.int32, shape, dim)


def dot(a, b, contract=((1,), (0,))):
    return lax.dot_general(a, b, (contract, ((), ())), preferred_element_type=F32)


def across(row, tall):
    return jnp.concatenate(
        [one_hot(tall == row[:, 128 * t : 128 * t + 128]) for t in range(row.shape[1] // 128)], axis=1
    )


def sorted_block(index):
    slot, rowmate, plane = index >> 7, (index >> 3) & 15, index & 7
    return (plane * ROWMATES + rowmate) * SLOTS + slot


def side_by_side(pieces):
    rows = pieces.astype(F32).reshape(ROWMATES, 4, PLANES, 128)
    return jnp.concatenate([rows[:, i].reshape(128, 128) for i in range(4)], axis=1).astype(BF16)


def kernel(
    grads_in, owner_in, left_stat, right_stat, left_root, right_root,
    new_left, new_right, total, last_spread, last_pieces,
    grads, owner, l_stat, r_stat, target, by_row, blocks, spread, stage,
    send_a, recv_a, send_b, g, roots, full, root_relay_0, root_relay_1, p, send_c, recv_c, send_d, recv_d,
    outer_send, outer_recv, outer_relay_0, outer_relay_1,
    local_sem, a_send, a_recv, b_send, b_recv, c_send, c_recv, d_send, d_recv,
    root_send, root_recv, root_relay_recv, outer_sent, outer_arrived, outer_relay_recv, members_in,
):
    d = lax.axis_index("dp")
    c = lax.axis_index("mp")
    plane = d // ROWMATES
    mate = d % ROWMATES
    right = lax.rem(c + 1, MEMBERS)
    left = lax.rem(c + MEMBERS - 1, MEMBERS)
    far = lax.rem(c + 2, MEMBERS)
    to_right, to_left = (d, right), (d, left)

    twice = 2 * lax.rem(d, 2)
    shift = lax.rem(twice + plane, MEMBERS)
    own_slot, right_slot, far_slot, left_slot = [lax.rem(c + i + MEMBERS - shift, MEMBERS) for i in range(MEMBERS)]

    def worker(k, owner_plane):
        return lax.rem(k + twice + owner_plane, MEMBERS)

    def far_first(j, count):
        return count // 2 + (j // 2) * (2 * (j % 2) - 1)

    def mate_at(j):
        other = lax.rem(mate + far_first(j, ROWMATES), ROWMATES)
        return other, plane * ROWMATES + other

    def plane_at(j):
        other = lax.rem(plane + far_first(j, PLANES), PLANES)
        return other, other * ROWMATES + mate

    def remote(src, dst, send, recv, device):
        return pltpu.make_async_remote_copy(
            src_ref=src, dst_ref=dst, send_sem=send, recv_sem=recv, device_id=device, device_id_type=MESH
        )

    def wait_bytes(ref, sem):
        pltpu.make_async_copy(ref, ref, sem).wait()

    def aligned(start, size):
        return pl.ds(pl.multiple_of(start, size), size)

    own = [
        pltpu.make_async_copy(owner_in, owner, local_sem.at[5]),
        pltpu.make_async_copy(grads_in, grads, local_sem.at[0]),
        pltpu.make_async_copy(left_root, roots.at[0], local_sem.at[1]),
        pltpu.make_async_copy(right_root, roots.at[1], local_sem.at[2]),
        pltpu.make_async_copy(left_stat, l_stat, local_sem.at[3]),
        pltpu.make_async_copy(right_stat, r_stat, local_sem.at[4]),
    ]
    for copy in own[:2]:
        copy.start()

    barrier = pltpu.get_barrier_semaphore()

    @pl.loop(1, ROWMATES, unroll=True)
    def _(j):
        pl.semaphore_signal(barrier, inc=1, device_id=(mate_at(j)[1], c), device_id_type=MESH)

    @pl.loop(1, MEMBERS, unroll=True)
    def _(j):
        pl.semaphore_signal(barrier, inc=1, device_id=(d, lax.rem(c + j, MEMBERS)), device_id_type=MESH)

    @pl.loop(1, PLANES, unroll=True)
    def _(j):
        pl.semaphore_signal(barrier, inc=1, device_id=(plane_at(j)[1], c), device_id_type=MESH)

    for copy in own[2:]:
        copy.start()

    def tell_column():
        @pl.loop(1, PLANES, unroll=True)
        def _(j):
            pl.semaphore_signal(members_in, inc=1, device_id=(plane_at(j)[1], c), device_id_type=MESH)

    top, bottom = pl.ds(0, VIA_RIGHT), pl.ds(VIA_RIGHT, 128 - VIA_RIGHT)

    def start_roots(k):
        @pl.when(far_slot == k)
        def _():
            remote(
                roots.at[:, k, top], root_relay_0, root_send.at[2], root_relay_recv.at[0], to_right
            ).start()
            remote(
                roots.at[:, k, bottom], root_relay_1, root_send.at[3], root_relay_recv.at[1], to_left
            ).start()

        @pl.when(right_slot == k)
        def _():
            remote(roots.at[:, k], full.at[:, c], root_send.at[0], root_recv, to_right).start()

        @pl.when(left_slot == k)
        def _():
            remote(roots.at[:, k], full.at[:, c], root_send.at[1], root_recv, to_left).start()

        @pl.when(own_slot == k)
        def _():
            full[:, c] = roots[:, k]

    def pass_roots(k):
        @pl.when(right_slot == k)
        def _():
            wait_bytes(root_relay_0, root_relay_recv.at[0])
            remote(root_relay_0, full.at[:, left, top], root_send.at[4], root_recv, to_right).start()

        @pl.when(left_slot == k)
        def _():
            wait_bytes(root_relay_1, root_relay_recv.at[1])
            remote(root_relay_1, full.at[:, right, bottom], root_send.at[5], root_recv, to_left).start()

    def make_a(k):
        wanted = sorted_block(iota((128, 128), 0) + 128 * k).astype(F32)
        moved = dot(across(target[0:1, :], wanted), blocks[...])
        rows = [moved[:, 128 * i : 128 * i + 128].reshape(ROWMATES, 1, PLANES, 128) for i in range(4)]
        send_a[k] = jnp.concatenate(rows, axis=1).reshape(ROWMATES, 32, 128).astype(BF16)

    def start_a(k):
        @pl.loop(1, ROWMATES, unroll=True)
        def _(j):
            other, device = mate_at(j)
            remote(send_a.at[k, other], recv_a.at[k, mate], a_send.at[k], a_recv.at[k], (device, c)).start()

        recv_a[k, mate] = send_a[k, mate]

    def start_b(k):
        wait_bytes(recv_a.at[k, pl.ds(0, ROWMATES - 1)], a_recv.at[k])
        stage[...] = recv_a[k].reshape(512, 128).astype(F32)
        for i in range(PLANES):
            send_b[k, i] = stage[pl.ds(i, 64, stride=PLANES), :].astype(BF16)
        member = worker(k, plane)
        place = c * PLANES + plane

        @pl.loop(1, PLANES, unroll=True)
        def _(j):
            other, device = plane_at(j)
            remote(send_b.at[k, other], g.at[place], b_send.at[k], b_recv, (device, worker(k, other))).start()

        @pl.when(member != c)
        def _():
            remote(send_b.at[k, plane], g.at[place], b_send.at[k], b_recv, (d, member)).start()

        @pl.when(member == c)
        def _():
            g[place] = send_b[k, plane]

    def gradient():
        parts = [g[pl.ds(PLANES * j, PLANES)].reshape(512, 128) for j in range(MEMBERS)]
        return jnp.concatenate(parts, axis=1)

    def work():
        wait_bytes(full.at[:, pl.ds(0, MEMBERS - 1)], root_recv)
        wait_bytes(g.at[pl.ds(0, PLANES * MEMBERS - 1)], b_recv)
        wide = gradient()
        half_way = dot(wide, full[1].reshape(512, 512)).astype(BF16)
        p[...] = dot(full[0].reshape(512, 512), half_way)
        grad_squares = jnp.zeros((1, 512), F32)
        product_squares = jnp.zeros((1, 512), F32)
        for i in range(4):
            part = wide[128 * i : 128 * i + 128].astype(F32)
            grad_squares = grad_squares + jnp.sum(part * part, axis=0, keepdims=True)
            part = p[pl.ds(128 * i, 128), :]
            product_squares = product_squares + jnp.sum(part * part, axis=0, keepdims=True)
        grad_squares = jnp.sum(grad_squares, axis=1, keepdims=True)
        product_squares = jnp.sum(product_squares, axis=1, keepdims=True)
        scale = jnp.sqrt(grad_squares / (product_squares + EPSILON))
        for j in range(MEMBERS):
            send_c[j] = (p[:, 128 * j : 128 * j + 128] * scale).astype(BF16).reshape(PLANES, 64, 128)

        for half in range(HALVES):
            rows = pl.ds(32 * half, 32)

            def send(member, other):
                remote(
                    send_c.at[member, other, rows], recv_c.at[own_slot, plane, rows],
                    c_send, c_recv.at[own_slot, half], (other * ROWMATES + mate, member),
                ).start()

            @pl.loop(0, (PLANES - 1) * MEMBERS, unroll=True)
            def _(j):
                send(lax.rem(c + 2 + j % MEMBERS, MEMBERS), plane_at(j // MEMBERS + 1)[0])

            @pl.loop(1, MEMBERS, unroll=True)
            def _(j):
                send(lax.rem(c + j, MEMBERS), plane)

        recv_c[own_slot, plane] = send_c[c, plane]

    def outer_products():
        wide = gradient()
        for i, axis in enumerate((1, 0)):
            outer_send[i] = dot(wide, wide, ((axis,), (axis,))).astype(BF16).reshape(MEMBERS, 128, 512)
            remote(
                outer_send.at[i, far, top], outer_relay_0.at[i], outer_sent.at[2], outer_relay_recv.at[0], to_right
            ).start()
            remote(
                outer_send.at[i, far, bottom], outer_relay_1.at[i], outer_sent.at[3], outer_relay_recv.at[1], to_left
            ).start()
            for number, (member, device) in enumerate(((right, to_right), (left, to_left))):
                remote(
                    outer_send.at[i, member], outer_recv.at[own_slot, i],
                    outer_sent.at[number], outer_arrived.at[own_slot], device,
                ).start()
        outer_recv[own_slot] = outer_send[:, c]

    def pass_outer(k):
        @pl.when(left_slot == k)
        def _():
            wait_bytes(outer_relay_0, outer_relay_recv.at[0])
            remote(
                outer_relay_0, outer_recv.at[k, :, top],
                outer_sent.at[4], outer_arrived.at[k], to_right,
            ).start()

        @pl.when(right_slot == k)
        def _():
            wait_bytes(outer_relay_1, outer_relay_recv.at[1])
            remote(
                outer_relay_1, outer_recv.at[k, :, bottom],
                outer_sent.at[5], outer_arrived.at[k], to_left,
            ).start()

    def statistics(k):
        @pl.when(worker(k, plane) != c)
        def _():
            wait_bytes(outer_recv.at[k], outer_arrived.at[k])

        new_left[k] = DECAY * l_stat[k] + (1.0 - DECAY) / 512 * outer_recv[k, 0].astype(F32)
        new_right[k] = DECAY * r_stat[k] + (1.0 - DECAY) / 512 * outer_recv[k, 1].astype(F32)

    def start_d(k):
        for half in range(HALVES):
            rows = pl.ds(32 * half, 32)

            @pl.when(worker(k, plane) != c)
            def _():
                wait_bytes(recv_c.at[k, :, rows], c_recv.at[k, half])

            @pl.when(worker(k, plane) == c)
            def _():
                wait_bytes(recv_c.at[k, pl.ds(0, PLANES - 1), rows], c_recv.at[k, half])

            for i in range(PLANES):
                stage[pl.ds(i, 32, stride=PLANES), :] = recv_c[k, i, rows].astype(F32)
            send_d[k, pl.ds(8 * half, 8)] = stage[pl.ds(0, 256), :].astype(BF16).reshape(8, 32, 128)

            @pl.loop(0, 8, unroll=True)
            def _(j):
                other = 8 * half + lax.rem(mate + 4 + j, 8)

                @pl.when(other != mate)
                def _():
                    device = (plane * ROWMATES + other, c)
                    remote(send_d.at[k, other], recv_d.at[k, mate], d_send.at[k], d_recv.at[k], device).start()

        recv_d[k, mate] = send_d[k, mate]

    def finish(k):
        wait_bytes(recv_d.at[k, pl.ds(0, ROWMATES - 1)], d_recv.at[k])
        part = dot(spread[:, 128 * k : 128 * k + 128], side_by_side(recv_d[k]))
        total[...] = part if k == 0 else part + total[...]

    own[0].wait()
    owned = jnp.concatenate([one_hot(owner[i : i + 1, :] == iota((128, 128), 0)) for i in range(3)], axis=1)
    earlier = iota((128, 384), 0).astype(F32) * SLOTS
    for i in range(3):
        earlier += dot(
            owned[:, 128 * i : 128 * i + 128], one_hot(iota((128, 384), 0) + 128 * i < iota((128, 384), 1))
        )
    number = jnp.sum(owned.astype(F32) * earlier, axis=0, keepdims=True)
    target[...] = jnp.broadcast_to(number, (8, 384))

    own[1].wait()
    by_row[...] = grads[...].astype(F32)
    for i in range(4):
        blocks[:, 128 * i : 128 * i + 128] = by_row[pl.ds(i, 384, stride=4), :].astype(BF16)
    make_a(0)
    own[2].wait()
    own[3].wait()
    pl.semaphore_wait(barrier, ROWMATES + MEMBERS + PLANES - 3)
    start_roots(0)
    start_a(0)
    tell_column()
    for k in (1, 2):
        start_roots(k)
        make_a(k)
        start_a(k)
    column = jnp.transpose(jnp.broadcast_to(target[0:1, :], (128, 384)))
    spread[...] = across(sorted_block(iota((1, 384), 1)).astype(F32), column)

    pl.semaphore_wait(members_in, PLANES - 1)
    for k in range(SLOTS):
        start_b(k)
        pass_roots(k)
    for copy in own[4:]:
        copy.wait()
    pl.when(own_slot < SLOTS)(work)
    pl.when(own_slot < SLOTS)(outer_products)
    for k in range(SLOTS):
        start_d(k)
        pass_outer(k)
    finish(0)
    finish(1)
    statistics(0)
    statistics(1)
    last_spread[...] = spread[:, 256:384]
    wait_bytes(recv_d.at[2, pl.ds(0, ROWMATES - 1)], d_recv.at[2])
    last_pieces[...] = recv_d[2]
    statistics(2)

    for k in range(SLOTS):
        wait_bytes(send_a.at[k, pl.ds(0, ROWMATES - 1)], a_send.at[k])
        wait_bytes(send_d.at[k, pl.ds(0, ROWMATES - 1)], d_send.at[k])

        @pl.when(worker(k, plane) != c)
        def _():
            wait_bytes(send_b.at[k], b_send.at[k])

        @pl.when(worker(k, plane) == c)
        def _():
            wait_bytes(send_b.at[k, pl.ds(0, PLANES - 1)], b_send.at[k])

    @pl.when(own_slot < SLOTS)
    def _():
        wait_bytes(g.at[pl.ds(0, PLANES * MEMBERS - 1)], c_send)
        for i in range(2):
            wait_bytes(outer_recv.at[0], outer_sent.at[i])
        wait_bytes(outer_relay_0, outer_sent.at[2])
        wait_bytes(outer_relay_1, outer_sent.at[3])

    @pl.when(right_slot < SLOTS)
    def _():
        wait_bytes(full.at[:, 0], root_send.at[0])
        wait_bytes(root_relay_0, root_send.at[4])
        wait_bytes(outer_relay_1, outer_sent.at[5])

    @pl.when(left_slot < SLOTS)
    def _():
        wait_bytes(full.at[:, 0], root_send.at[1])
        wait_bytes(root_relay_1, root_send.at[5])
        wait_bytes(outer_relay_0, outer_sent.at[4])

    @pl.when(far_slot < SLOTS)
    def _():
        wait_bytes(root_relay_0, root_send.at[2])
        wait_bytes(root_relay_1, root_send.at[3])


def last_kernel(
    new_left, new_right, total, last_spread, last_pieces, left_out, right_out, precond_out, by_row, precond, sem
):
    copies = [
        pltpu.make_async_copy(source.at[k], result.at[k], sem.at[3 * i + k])
        for i, (source, result) in enumerate(((new_left, left_out), (new_right, right_out)))
        for k in range(SLOTS)
    ]
    for copy in copies:
        copy.start()
    blocks = total[...] + dot(last_spread[...], side_by_side(last_pieces[...]))
    for i in range(4):
        by_row[pl.ds(i, 384, stride=4), :] = blocks[:, 128 * i : 128 * i + 128]
    precond[...] = by_row[...].astype(BF16)
    copies.append(pltpu.make_async_copy(precond, precond_out, sem.at[6]))
    copies[-1].start()
    for copy in copies:
        copy.wait()


def local(grads, owner, left_stat, right_stat, left_root, right_root):
    any_space = pl.BlockSpec(memory_space=pl.ANY)
    vmem = pl.BlockSpec(memory_space=pltpu.VMEM)
    dma = pltpu.SemaphoreType.DMA
    results = pl.pallas_call(
        kernel,
        out_shape=(
            pltpu.VMEM((3, 128, 512), F32),
            pltpu.VMEM((3, 128, 512), F32),
            pltpu.VMEM((384, 512), F32),
            pltpu.VMEM((384, 128), BF16),
            pltpu.VMEM((16, 32, 128), BF16),
        ),
        in_specs=[any_space] * 6,
        out_specs=(vmem,) * 5,
        scratch_shapes=[
            pltpu.VMEM((1536, 128), BF16),
            pltpu.VMEM((3, 128), jnp.int32),
            pltpu.VMEM((3, 128, 512), F32),
            pltpu.VMEM((3, 128, 512), F32),
            pltpu.VMEM((8, 384), F32),
            pltpu.VMEM((1536, 128), F32),
            pltpu.VMEM((384, 512), BF16),
            pltpu.VMEM((384, 384), BF16),
            pltpu.VMEM((512, 128), F32),
            pltpu.VMEM((3, 16, 32, 128), BF16),
            pltpu.VMEM((3, 16, 32, 128), BF16),
            pltpu.VMEM((3, 8, 64, 128), BF16),
            pltpu.VMEM((32, 64, 128), BF16),
            pltpu.VMEM((2, 3, 128, 512), BF16),
            pltpu.VMEM((2, 4, 128, 512), BF16),
            pltpu.VMEM((2, VIA_RIGHT, 512), BF16),
            pltpu.VMEM((2, 128 - VIA_RIGHT, 512), BF16),
            pltpu.VMEM((512, 512), F32),
            pltpu.VMEM((4, 8, 64, 128), BF16),
            pltpu.VMEM((3, 8, 64, 128), BF16),
            pltpu.VMEM((3, 16, 32, 128), BF16),
            pltpu.VMEM((3, 16, 32, 128), BF16),
            pltpu.VMEM((2, 4, 128, 512), BF16),
            pltpu.VMEM((3, 2, 128, 512), BF16),
            pltpu.VMEM((2, VIA_RIGHT, 512), BF16),
            pltpu.VMEM((2, 128 - VIA_RIGHT, 512), BF16),
            dma((6,)),
            dma((3,)), dma((3,)),
            dma((3,)), dma,
            dma, dma((3, 2)),
            dma((3,)), dma((3,)),
            dma((6,)), dma, dma((2,)),
            dma((6,)), dma((3,)), dma((2,)),
            pltpu.SemaphoreType.REGULAR,
        ],
        compiler_params=pltpu.CompilerParams(
            collective_id=0, has_side_effects=True, vmem_limit_bytes=58 * 1024 * 1024
        ),
        cost_estimate=pl.CostEstimate(flops=4_000_000_000, bytes_accessed=6_000_000, transcendentals=0),
    )(grads.reshape(1536, 128), owner.reshape(3, 128), left_stat, right_stat, left_root, right_root)
    new_left, new_right, precond = pl.pallas_call(
        last_kernel,
        out_shape=(
            jax.ShapeDtypeStruct((3, 128, 512), F32),
            jax.ShapeDtypeStruct((3, 128, 512), F32),
            jax.ShapeDtypeStruct((1536, 128), BF16),
        ),
        in_specs=[vmem] * 5,
        out_specs=(any_space,) * 3,
        scratch_shapes=[pltpu.VMEM((1536, 128), F32), pltpu.VMEM((1536, 128), BF16), dma((7,))],
        compiler_params=pltpu.CompilerParams(vmem_limit_bytes=4 * 1024 * 1024),
        cost_estimate=pl.CostEstimate(flops=0, bytes_accessed=4_000_000, transcendentals=0),
    )(*results)
    return new_left, new_right, precond.reshape(384, 4, 128)


def solution(mesh):
    in_specs = (
        P(None, "dp", "mp"),
        P(),
        P("dp", "mp", None),
        P("dp", "mp", None),
        P("dp", "mp", None),
        P("dp", "mp", None),
    )
    out_specs = (P("dp", "mp", None), P("dp", "mp", None), P(None, "dp", "mp"))
    return jax.shard_map(local, mesh=mesh, in_specs=in_specs, out_specs=out_specs, check_vma=False)
```
